512 devices in a mesh: inst: 128 (over y, z, core), tp: 4 (over x).
Axes of the slice: x: 4, y: 8, z: 8, core: 2. Of those that a mesh axis runs over, the one named last changes fastest.
Arguments:
- queries: bfloat16 [256, 4, 2560], P('inst', None, 'tp'), may hold values from -512 to 512
- new_keys: bfloat16 [256, 4, 512], P('inst', None, 'tp'), may hold values from -6 to 6
- new_values: bfloat16 [256, 4, 512], P('inst', None, 'tp'), may hold values from -24 to 24
- res_keys: bfloat16 [256, 512, 512], P('inst', None, 'tp'), may hold values from -6 to 6
- res_values: bfloat16 [256, 512, 512], P('inst', None, 'tp'), may hold values from -24 to 24
- lendable_keys: bfloat16 [1024, 128, 512], P('inst', None, 'tp'), may hold values from -6 to 6
- lendable_values: bfloat16 [1024, 128, 512], P('inst', None, 'tp'), may hold values from -24 to 24
- ctx_len: int32 [256], P('inst'), may hold values from 256 to 1024, as said below
- blocks: int32 [256, 4], P('inst'), may hold values from 0 to 7, as said below
- lender: int32 [128], replicated, may hold values from 0 to 127, as said below
- out_proj: bfloat16 [2560, 2560], P('tp'), may hold values from -0.625 to 0.625
Outputs:
- layer_out: bfloat16 [256, 4, 2560], P('inst', None, 'tp')
The draws below stay inside these ranges and needn't reach their ends.
Inputs may be any that keep to these rules, and one draw needn't show every extreme that they name: The first min(ctx_len, 512) tokens of a request sit in its resident cache, the rest in ceil((ctx_len - 512) / 128) lent blocks, all full but the last; the largest value is reached. The 2 lists of one instance together name every pool slot 0 to 7 once; a request's lent blocks are the first entries of its list in order of its tokens. `lender`: a permutation of the instances that forms one cycle through all of them.
All inputs are finite; a program needn't handle non-finite values.
Results may differ from the reference program's by a relative error of at most 0.0051.
Values may be sent and summed in bfloat16 or wider, within the bound.
No kernel may reach another device: no remote copies, remote signals or barrier semaphores. Data moves between devices by JAX's collectives and lax.ppermute only.
A program may use at most 64 MiB of HBM per device.

```python
import math
import jax
import jax.numpy as jnp
from jax import lax

HEAD_SIZE = 128
QH = 20
KEY_VALUE_HEADS = 4
OUTW = 2560
BLOCK_TOKENS = 128
ROWS = 2
STEPS = 4
POOL = 8
GROUP = 5
RES_CAP = 512
LENT_MAX = 4
MINCTX = 256
MAXCTX = 1024
NINST = 128
NREQ = 256
LENDABLE_BLOCKS = 1024


def base_resident(key):
    return jnp.clip(jax.random.normal(jax.random.fold_in(key, 101), (NREQ, RES_CAP, KEY_VALUE_HEADS * HEAD_SIZE), jnp.float32), -6.0, 6.0)


def base_fresh(key):
    return jnp.clip(jax.random.normal(jax.random.fold_in(key, 102), (NREQ, STEPS, KEY_VALUE_HEADS * HEAD_SIZE), jnp.float32), -6.0, 6.0)


def draw_res_keys(key, part):
    shared = base_resident(key)
    return shared.astype(jnp.bfloat16)


def draw_new_keys(key, part):
    shared = base_fresh(key)
    return shared.astype(jnp.bfloat16)


def draw_queries(key, part):
    fresh = base_fresh(key)
    key = jax.random.fold_in(key, 3)
    noise_key = jax.random.fold_in(key, 0)
    noise_part = jnp.clip(jax.random.normal(noise_key, (NREQ, STEPS, QH * HEAD_SIZE), jnp.float32), -4.0, 4.0)
    own_key = jnp.broadcast_to(fresh.reshape(NREQ, STEPS, KEY_VALUE_HEADS, 1, HEAD_SIZE), (NREQ, STEPS, KEY_VALUE_HEADS, GROUP, HEAD_SIZE)).reshape(NREQ, STEPS, QH * HEAD_SIZE)
    drawn_query = noise_part + 0.4 * own_key
    return jnp.clip(drawn_query, -512.0, 512.0).astype(jnp.bfloat16)


def draw_lender(key, part):
    key = jax.random.fold_in(key, 4)
    ordering = jax.random.permutation(key, NINST).astype(jnp.int32)
    cycle_next = jnp.roll(ordering, -1)
    return jnp.zeros((NINST,), jnp.int32).at[ordering].set(cycle_next)


def draw_blocks(key, part):
    key = jax.random.fold_in(key, 5)
    order_scores = jax.random.randint(key, (NINST, POOL), 0, 1 << 20) * POOL + jnp.arange(POOL, dtype=jnp.int32)[None, :]
    ordering = jnp.argsort(order_scores, axis=1, stable=True).astype(jnp.int32)
    return ordering.reshape(NREQ, LENT_MAX)


def draw_ctx_len(key, part):
    key = jax.random.fold_in(key, 6)
    lengths = jax.random.randint(key, (NREQ,), MINCTX, MAXCTX + 1).astype(jnp.int32)
    return lengths.at[0].set(MAXCTX)


def spiked(values, rng, source, target, blocks, factor):
    def block_of(dim):
        return (jnp.arange(values.shape[dim]) // (values.shape[dim] // blocks)).reshape((-1,) + (1,) * (values.ndim - 1 - dim))

    first = jax.random.permutation(rng, blocks)[block_of(target)]
    far = (block_of(target) + blocks // 2) % blocks
    return jnp.where((block_of(source) == first) | (block_of(source) == far), factor * values, values)


def steps_of(rng, extent, shards, low, largest):
    def one(position, shards_of):
        draws = jax.random.uniform(jax.random.fold_in(jax.random.fold_in(rng, 6), position), (shards_of,), jnp.float32, low / len(shards), largest / len(shards))
        return jnp.repeat(jnp.exp(draws), extent[position] // shards_of).reshape((-1,) + (1,) * (len(extent) - position - 1))

    gain = one(*shards[0])
    for cut in shards[1:]:
        gain = gain * one(*cut)
    return gain


def noise(key, extent, spread, bound, cuts=(), held_as=jnp.bfloat16):
    result = spread * jax.random.normal(key, extent, jnp.float32)
    if cuts:
        result = result * steps_of(key, extent, cuts, -0.22, 0.18)
    return jnp.clip(result, -bound, bound).astype(held_as)


def noise_with(rng, extent, scale, reach, pieces, heavy, kind=jnp.bfloat16):
    values = scale * jax.random.normal(rng, extent, jnp.float32)
    if pieces:
        values = values * steps_of(rng, extent, pieces, -0.22, 0.18)
    return jnp.clip(spiked(values, jax.random.fold_in(rng, 3), *heavy), -reach, reach).astype(kind)


def setup_inputs(seed: int = 0) -> dict:
    seeds = jax.random.split(jax.random.key(seed), 12)
    queries = draw_queries(jax.random.fold_in(seeds[11], 71), 0)
    new_keys = draw_new_keys(jax.random.fold_in(seeds[11], 71), 0)
    new_values = noise(seeds[2], (NREQ, STEPS, KEY_VALUE_HEADS * HEAD_SIZE), 4.0, 24.0, ((0, 128), (2, 4)))
    res_keys = draw_res_keys(jax.random.fold_in(seeds[11], 71), 0)
    res_values = noise(seeds[4], (NREQ, RES_CAP, KEY_VALUE_HEADS * HEAD_SIZE), 4.0, 24.0, ((0, 128), (2, 4)))
    lendable_keys = noise(seeds[5], (LENDABLE_BLOCKS, BLOCK_TOKENS, KEY_VALUE_HEADS * HEAD_SIZE), 1.0, 6.0, ((0, 128), (2, 4)))
    lendable_values = noise(seeds[6], (LENDABLE_BLOCKS, BLOCK_TOKENS, KEY_VALUE_HEADS * HEAD_SIZE), 4.0, 24.0, ((0, 128), (2, 4)))
    ctx_len = draw_ctx_len(jax.random.fold_in(seeds[11], 71), 0)
    blocks = draw_blocks(jax.random.fold_in(seeds[11], 71), 0)
    lender = draw_lender(jax.random.fold_in(seeds[11], 71), 0)
    out_proj = noise_with(seeds[10], (QH * HEAD_SIZE, OUTW), (QH * HEAD_SIZE // 16) ** -0.5, 0.625, ((0, 4),), (0, 1, 4, 2.0))
    return dict(queries=queries, new_keys=new_keys, new_values=new_values, res_keys=res_keys, res_values=res_values, lendable_keys=lendable_keys, lendable_values=lendable_values, ctx_len=ctx_len, blocks=blocks, lender=lender, out_proj=out_proj)


big_negative = -1e+30

def masked_max(scores, valid):
    return lax.optimization_barrier(jnp.max(jnp.where(valid, scores, big_negative), axis=-1))

def masked_weights(scores, valid, joint_max):
    return jnp.where(valid, jnp.exp(jnp.where(valid, scores, big_negative) - joint_max[..., None]), 0.0)

def rounded_length(weights):
    return lax.optimization_barrier(weights.astype(jnp.bfloat16)).astype(jnp.float32)

def reference(queries, new_keys, new_values, res_keys, res_values, lendable_keys, lendable_values, ctx_len, blocks, lender, out_proj):
    score_scale = 1.0 / math.sqrt(HEAD_SIZE)

    def request(index):
        context_window = ctx_len[index]
        query_heads = queries[index].astype(jnp.float32).reshape(STEPS, KEY_VALUE_HEADS, GROUP, HEAD_SIZE)
        resident_k = res_keys[index].astype(jnp.float32).reshape(RES_CAP, KEY_VALUE_HEADS, HEAD_SIZE)
        resident_v = res_values[index].astype(jnp.float32).reshape(RES_CAP, KEY_VALUE_HEADS, HEAD_SIZE)
        fresh_k = new_keys[index].astype(jnp.float32).reshape(STEPS, KEY_VALUE_HEADS, HEAD_SIZE)
        fresh_v = new_values[index].astype(jnp.float32).reshape(STEPS, KEY_VALUE_HEADS, HEAD_SIZE)
        slots = (lender[index // ROWS] * POOL + blocks[index]).astype(jnp.int32)
        lent_k = lendable_keys[slots].astype(jnp.float32).reshape(LENT_MAX * BLOCK_TOKENS, KEY_VALUE_HEADS, HEAD_SIZE)
        lent_v = lendable_values[slots].astype(jnp.float32).reshape(LENT_MAX * BLOCK_TOKENS, KEY_VALUE_HEADS, HEAD_SIZE)
        res_scores = jnp.einsum('sgjd,tgd->sgjt', query_heads, resident_k) * score_scale
        new_scores = jnp.einsum('sgjd,ugd->sgju', query_heads, fresh_k) * score_scale
        lent_scores = jnp.einsum('sgjd,tgd->sgjt', query_heads, lent_k) * score_scale
        res_valid = (jnp.arange(RES_CAP) < jnp.minimum(context_window, RES_CAP))[None, None, None, :]
        new_valid = (jnp.arange(STEPS)[None, :] <= jnp.arange(STEPS)[:, None])[:, None, None, :]
        fill_counts = jnp.clip(context_window - RES_CAP - jnp.arange(LENT_MAX) * BLOCK_TOKENS, 0, BLOCK_TOKENS)
        lent_valid = (jnp.arange(BLOCK_TOKENS)[None, :] < fill_counts[:, None]).reshape(LENT_MAX * BLOCK_TOKENS)[None, None, None, :]
        local_max = jnp.maximum(masked_max(res_scores, res_valid), masked_max(new_scores, new_valid))
        res_weights = masked_weights(res_scores, res_valid, local_max)
        new_weights = masked_weights(new_scores, new_valid, local_max)
        local_total = lax.optimization_barrier(jnp.sum(res_weights, axis=-1)) + lax.optimization_barrier(jnp.sum(new_weights, axis=-1))
        local_sum = jnp.einsum('sgjt,tgd->sgjd', rounded_length(res_weights), resident_v) + jnp.einsum('sgju,ugd->sgjd', rounded_length(new_weights), fresh_v)
        lent_max = masked_max(lent_scores, lent_valid)
        lent_weights = masked_weights(lent_scores, lent_valid, lent_max)
        lent_total = lax.optimization_barrier(jnp.sum(lent_weights, axis=-1))
        lent_sum = jnp.einsum('sgjt,tgd->sgjd', rounded_length(lent_weights), lent_v)
        joint_max = jnp.maximum(local_max, lent_max)
        local_factor = jnp.exp(local_max - joint_max)
        lent_factor = jnp.exp(lent_max - joint_max)
        numerator = local_factor[..., None] * local_sum + lent_factor[..., None] * lent_sum
        denominator = local_factor * local_total + lent_factor * lent_total
        attended = numerator / denominator[..., None]
        return attended.astype(jnp.bfloat16).reshape(STEPS, QH * HEAD_SIZE)
    attended = lax.map(request, jnp.arange(NREQ, dtype=jnp.int32))
    layer_out = jnp.dot(attended.reshape(NREQ * STEPS, QH * HEAD_SIZE), out_proj, preferred_element_type=jnp.float32)
    return layer_out.astype(jnp.bfloat16).reshape(NREQ, STEPS, OUTW)
```

```python
import functools
import math

import jax
import jax.numpy as jnp
from jax import lax
from jax.experimental import pallas as pl
from jax.experimental.pallas import tpu as pltpu
from jax.sharding import PartitionSpec as P

HEAD = 128
GROUP = 5
ROWS = 2
STEPS = 4
TILE = ROWS * STEPS
QROWS = GROUP * TILE
MSG = 48
LOW = -1e30
PARTS_M = 3
PARTS_L = 2
PER_HEAD = PARTS_M + PARTS_L
SCALE = 1.0 / math.sqrt(HEAD)
F32 = jnp.float32
BF16 = jnp.bfloat16

VMEM = pl.BlockSpec(memory_space=pltpu.VMEM)
SMEM = pl.BlockSpec(memory_space=pltpu.SMEM)


def call(kernel, outs, specs, limit=32 * 1024 * 1024):
    return pl.pallas_call(
        kernel,
        out_shape=outs,
        in_specs=specs,
        out_specs=jax.tree.map(lambda _: VMEM, outs),
        compiler_params=pltpu.CompilerParams(vmem_limit_bytes=limit),
    )


def head_rows(q_ref):
    q = jnp.concatenate([q_ref[r].astype(F32) for r in range(ROWS)], axis=0)
    return jnp.concatenate([q[:, h * HEAD : (h + 1) * HEAD] for h in range(GROUP)], axis=0)


def tile_iota(dim):
    return lax.broadcasted_iota(jnp.int32, (TILE, HEAD), dim)


def per_head(tile):
    return jnp.concatenate([tile] * GROUP, axis=0)


def pack_kernel(res_len, block_len, ctx_ref, blocks_ref, q_ref, out_ref):
    rows = head_rows(q_ref)
    side = jnp.zeros((TILE, HEAD), F32)
    request, lane = tile_iota(0) // STEPS, tile_iota(1)
    for r in range(ROWS):
        for i in range(blocks_ref.shape[1]):
            fill = jnp.clip(ctx_ref[r] - res_len - i * block_len, 0, block_len)
            hit = (request == r) & (lane == blocks_ref[r, i])
            side = jnp.where(hit, fill.astype(F32), side)
    message = jnp.concatenate([rows, side], axis=0).astype(BF16)
    for i in range(out_ref.shape[0]):
        out_ref[i] = message


def soft_part(scores, valid):
    masked = [jnp.where(v, s, LOW) for s, v in zip(scores, valid)]
    tops = [jnp.max(s, axis=1, keepdims=True) for s in masked]
    top = functools.reduce(jnp.maximum, tops)
    weights = [jnp.where(v, jnp.exp(s - top), 0.0) for s, v in zip(masked, valid)]
    total = sum(jnp.sum(w, axis=1, keepdims=True) for w in weights)
    return top, total, weights


def dot_t(a, b):
    return lax.dot_general(a, b, (((1,), (1,)), ((), ())), preferred_element_type=F32)


def home_kernel(ctx_ref, q_ref, nk_ref, nv_ref, k_ref, v_ref, o_ref, m_ref, l_ref):
    q = head_rows(q_ref).astype(BF16)
    res_len = k_ref.shape[1]
    request, step = tile_iota(0) // STEPS, tile_iota(0) % STEPS
    scores, valid = [], []
    for r in range(ROWS):
        s = dot_t(q, k_ref[r]) * SCALE
        for c in range(res_len // HEAD):
            scores.append(s[:, c * HEAD : (c + 1) * HEAD])
            valid.append(per_head((request == r) & (tile_iota(1) + c * HEAD < ctx_ref[r])))
    fill = jnp.zeros((HEAD - TILE, HEAD), F32)

    def fresh(ref):
        return jnp.concatenate([ref[r].astype(F32) for r in range(ROWS)] + [fill], axis=0)

    scores.append(dot_t(q, fresh(nk_ref).astype(BF16)) * SCALE)
    lane = tile_iota(1)
    valid.append(
        per_head((lane < TILE) & (lane // STEPS == request) & (lane % STEPS <= step))
    )
    top, total, weights = soft_part(scores, valid)
    w = [x.astype(BF16) for x in weights]
    acc = jnp.dot(w[-1], fresh(nv_ref).astype(BF16), preferred_element_type=F32)
    per = res_len // HEAD
    for r in range(ROWS):
        wide = jnp.concatenate(w[r * per : (r + 1) * per], axis=1)
        acc = acc + jnp.dot(wide, v_ref[r], preferred_element_type=F32)
    o_ref[...] = acc
    m_ref[...] = jnp.broadcast_to(top, m_ref.shape)
    l_ref[...] = jnp.broadcast_to(total, l_ref.shape)


def place_out_kernel(per_row, lender_ref, me_ref, in_ref, out_ref):
    my_row, my_col = me_ref[0] // per_row, me_ref[0] % per_row
    out_ref[...] = jnp.zeros_like(out_ref)
    for y in range(in_ref.shape[0]):
        target = lender_ref[y * per_row + my_col]

        @pl.when(target // per_row == my_row)
        def _():
            out_ref[target % per_row] = in_ref[y]


def place_back_kernel(per_row, lender_ref, me_ref, in_ref, out_ref):
    my_row, my_col = me_ref[0] // per_row, me_ref[0] % per_row
    for y in range(out_ref.shape[0]):
        source = lender_ref[y * per_row + my_col]
        mine = source // per_row == my_row

        @pl.when(mine)
        def _():
            out_ref[y] = in_ref[source % per_row]

        @pl.when(jnp.logical_not(mine))
        def _():
            out_ref[y] = jnp.zeros(out_ref.shape[1:], BF16)


def merged(in_ref):
    total = in_ref[0].astype(F32)
    for i in range(1, in_ref.shape[0]):
        total = total + in_ref[i].astype(F32)
    return total


def pieces(x, count):
    found = []
    for _ in range(count):
        piece = x.astype(BF16).astype(F32)
        found.append(piece)
        x = x - piece
    return found


def lent_kernel(in_ref, k_ref, v_ref, out_ref):
    message = merged(in_ref)
    q = message[:QROWS].astype(BF16)
    fills = message[QROWS:]
    block_len = k_ref.shape[1]
    k = k_ref[...].reshape(-1, HEAD)
    v = v_ref[...].reshape(-1, HEAD)
    s = dot_t(q, k) * SCALE
    lane = tile_iota(1).astype(F32)
    scores, valid = [], []
    for p in range(k_ref.shape[0]):
        scores.append(s[:, p * block_len : (p + 1) * block_len])
        valid.append(per_head(lane < fills[:, p : p + 1]))
    top, total, weights = soft_part(scores, valid)
    wide = jnp.concatenate([w.astype(BF16) for w in weights], axis=1)
    acc = jnp.dot(wide, v, preferred_element_type=F32)
    acc = acc * jnp.where(total > 0.0, 1.0 / jnp.maximum(total, 1e-30), 0.0)
    side = jnp.zeros((TILE, HEAD), F32)
    for h in range(GROUP):
        span = slice(h * TILE, (h + 1) * TILE)
        values = pieces(top[span], PARTS_M) + pieces(total[span], PARTS_L)
        for i, value in enumerate(values):
            side = jnp.where(tile_iota(1) == h * PER_HEAD + i, value, side)
    reply = jnp.concatenate([acc, side], axis=0).astype(BF16)
    for i in range(out_ref.shape[0]):
        out_ref[i] = reply


def project_kernel(in_ref, o_ref, m_ref, l_ref, w_ref, out_ref):
    reply = merged(in_ref)
    side = reply[QROWS:]
    heads = []
    for h in range(GROUP):
        span = slice(h * TILE, (h + 1) * TILE)
        cols = [side[:, h * PER_HEAD + i : h * PER_HEAD + i + 1] for i in range(PER_HEAD)]
        lent_top = cols[0] + cols[1] + cols[2]
        lent_total = cols[3] + cols[4]
        top = jnp.maximum(m_ref[span], lent_top)
        a = jnp.exp(m_ref[span] - top)
        b = jnp.exp(lent_top - top) * lent_total
        mixed = (a * o_ref[span] + b * reply[span]) / (a * l_ref[span] + b)
        heads.append(mixed.astype(BF16))
    attended = jnp.concatenate(heads, axis=1)
    width = out_ref.shape[2]
    for i in range(out_ref.shape[0]):
        out_ref[i] = jnp.dot(
            attended, w_ref[:, i * width : (i + 1) * width], preferred_element_type=F32
        )


def solution(mesh):
    insts, shards = mesh.shape["inst"], mesh.shape["tp"]
    per_row = 16
    lines = insts // per_row
    along_y = [[y * per_row + c for y in range(lines)] for c in range(per_row)]
    along_row = [[y * per_row + c for c in range(per_row)] for y in range(lines)]

    def exchange(x, groups):
        return lax.all_to_all(x, "inst", 0, 0, axis_index_groups=groups, tiled=True)

    def local(
        queries,
        new_keys,
        new_values,
        res_keys,
        res_values,
        lendable_keys,
        lendable_values,
        ctx_len,
        blocks,
        lender,
        out_proj,
    ):
        me = lax.axis_index("inst").astype(jnp.int32).reshape(1)

        def slots(n):
            return jax.ShapeDtypeStruct((n, MSG, HEAD), BF16)

        pack = functools.partial(pack_kernel, res_keys.shape[1], lendable_keys.shape[1])
        sent = call(pack, slots(lines), [SMEM, SMEM, VMEM])(ctx_len, blocks, queries)
        held = exchange(sent, along_y)
        part = jax.ShapeDtypeStruct((QROWS, HEAD), F32)
        home = call(home_kernel, (part, part, part), [SMEM] + [VMEM] * 5)(
            ctx_len, queries, new_keys, new_values, res_keys, res_values
        )
        place_out = functools.partial(place_out_kernel, per_row)
        placed = call(place_out, slots(per_row), [SMEM, SMEM, VMEM])(lender, me, held)
        arrived = exchange(placed, along_row)
        reply = call(lent_kernel, slots(per_row), [VMEM] * 3)(
            arrived, lendable_keys, lendable_values
        )
        held_back = exchange(reply, along_row)
        place_back = functools.partial(place_back_kernel, per_row)
        placed_back = call(place_back, slots(lines), [SMEM, SMEM, VMEM])(lender, me, held_back)
        returned = exchange(placed_back, along_y)
        width = out_proj.shape[1] // shards
        terms = call(
            project_kernel,
            jax.ShapeDtypeStruct((shards, TILE, width), F32),
            [VMEM] * 5,
        )(returned, *home, out_proj)
        shares = lax.all_to_all(terms, "tp", 0, 0, tiled=True)
        return jnp.sum(shares, axis=0).astype(BF16).reshape(ROWS, STEPS, width)

    in_specs = (
        P("inst", None, "tp"),
        P("inst", None, "tp"),
        P("inst", None, "tp"),
        P("inst", None, "tp"),
        P("inst", None, "tp"),
        P("inst", None, "tp"),
        P("inst", None, "tp"),
        P("inst"),
        P("inst", None),
        P(),
        P("tp", None),
    )
    out_specs = P("inst", None, "tp")
    return jax.shard_map(local, mesh=mesh, in_specs=in_specs, out_specs=out_specs, check_vma=False)
```

```python
import functools
import math

import jax
import jax.numpy as jnp
from jax import lax
from jax.experimental import pallas as pl
from jax.experimental.pallas import tpu as pltpu
from jax.sharding import PartitionSpec as P

HEAD = 128
GROUP = 5
ROWS = 2
STEPS = 4
TILE = ROWS * STEPS
QROWS = GROUP * TILE
MSG = 48
LOW = -1e30
PARTS_M = 3
PARTS_L = 2
PER_HEAD = PARTS_M + PARTS_L
SCALE = 1.0 / math.sqrt(HEAD)
F32 = jnp.float32
BF16 = jnp.bfloat16

VMEM = pl.BlockSpec(memory_space=pltpu.VMEM)
SMEM = pl.BlockSpec(memory_space=pltpu.SMEM)
HBM = pl.BlockSpec(memory_space=pltpu.HBM)


def off_chip(x):
    return pltpu.with_memory_space_constraint(x, pltpu.HBM)


def call(kernel, outs, specs, scratch=(), limit=32 * 1024 * 1024):
    return pl.pallas_call(
        kernel,
        out_shape=outs,
        in_specs=specs,
        out_specs=jax.tree.map(lambda _: VMEM, outs),
        scratch_shapes=scratch,
        compiler_params=pltpu.CompilerParams(vmem_limit_bytes=limit),
    )


def head_rows(q_ref):
    q = jnp.concatenate([q_ref[r].astype(F32) for r in range(ROWS)], axis=0)
    return jnp.concatenate([q[:, h * HEAD : (h + 1) * HEAD] for h in range(GROUP)], axis=0)


def fetch(pairs, sems):
    copies = [pltpu.make_async_copy(s, d, sems.at[i]) for i, (s, d) in enumerate(pairs)]
    for copy in copies:
        copy.start()
    return copies


def tile_iota(dim):
    return lax.broadcasted_iota(jnp.int32, (TILE, HEAD), dim)


def per_head(tile):
    return jnp.concatenate([tile] * GROUP, axis=0)


def pack_kernel(
    res_len, block_len, ctx_hbm, blocks_hbm, q_hbm, out_ref, ctx_ref, blocks_ref, q_ref, sems
):
    pairs = [(q_hbm, q_ref), (ctx_hbm, ctx_ref), (blocks_hbm, blocks_ref)]
    for copy in fetch(pairs, sems):
        copy.wait()
    rows = head_rows(q_ref)
    side = jnp.zeros((TILE, HEAD), F32)
    request, lane = tile_iota(0) // STEPS, tile_iota(1)
    for r in range(ROWS):
        for i in range(blocks_ref.shape[1]):
            fill = jnp.clip(ctx_ref[r] - res_len - i * block_len, 0, block_len)
            hit = (request == r) & (lane == blocks_ref[r, i])
            side = jnp.where(hit, fill.astype(F32), side)
    message = jnp.concatenate([rows, side], axis=0).astype(BF16)
    for i in range(out_ref.shape[0]):
        out_ref[i] = message


def soft_part(scores, valid):
    masked = [jnp.where(v, s, LOW) for s, v in zip(scores, valid)]
    tops = [jnp.max(s, axis=1, keepdims=True) for s in masked]
    top = functools.reduce(jnp.maximum, tops)
    weights = [jnp.where(v, jnp.exp(s - top), 0.0) for s, v in zip(masked, valid)]
    total = sum(jnp.sum(w, axis=1, keepdims=True) for w in weights)
    return top, total, weights


def dot_t(a, b):
    return lax.dot_general(a, b, (((1,), (1,)), ((), ())), preferred_element_type=F32)


def home_kernel(
    ctx_hbm,
    q_hbm,
    nk_hbm,
    nv_hbm,
    k_hbm,
    v_hbm,
    lk_hbm,
    lv_hbm,
    lender_hbm,
    o_ref,
    m_ref,
    l_ref,
    lk_ref,
    lv_ref,
    lender_ref,
    ctx_ref,
    q_ref,
    nk_ref,
    nv_ref,
    k_ref,
    v_ref,
    sems,
):
    pairs = [
        (ctx_hbm, ctx_ref),
        (q_hbm, q_ref),
        (nk_hbm, nk_ref),
        (k_hbm, k_ref),
        (v_hbm, v_ref),
        (nv_hbm, nv_ref),
        (lender_hbm, lender_ref),
        (lk_hbm, lk_ref),
        (lv_hbm, lv_ref),
    ]
    for copy in fetch(pairs, sems):
        copy.wait()
    q = head_rows(q_ref).astype(BF16)
    res_len = k_ref.shape[1]
    request, step = tile_iota(0) // STEPS, tile_iota(0) % STEPS
    scores, valid = [], []
    for r in range(ROWS):
        s = dot_t(q, k_ref[r]) * SCALE
        for c in range(res_len // HEAD):
            scores.append(s[:, c * HEAD : (c + 1) * HEAD])
            valid.append(per_head((request == r) & (tile_iota(1) + c * HEAD < ctx_ref[r])))
    fill = jnp.zeros((HEAD - TILE, HEAD), F32)

    def fresh(ref):
        return jnp.concatenate([ref[r].astype(F32) for r in range(ROWS)] + [fill], axis=0)

    scores.append(dot_t(q, fresh(nk_ref).astype(BF16)) * SCALE)
    lane = tile_iota(1)
    valid.append(
        per_head((lane < TILE) & (lane // STEPS == request) & (lane % STEPS <= step))
    )
    top, total, weights = soft_part(scores, valid)
    w = [x.astype(BF16) for x in weights]
    acc = jnp.dot(w[-1], fresh(nv_ref).astype(BF16), preferred_element_type=F32)
    per = res_len // HEAD
    for r in range(ROWS):
        wide = jnp.concatenate(w[r * per : (r + 1) * per], axis=1)
        acc = acc + jnp.dot(wide, v_ref[r], preferred_element_type=F32)
    o_ref[...] = acc
    m_ref[...] = jnp.broadcast_to(top, m_ref.shape)
    l_ref[...] = jnp.broadcast_to(total, l_ref.shape)


def place_out_kernel(per_row, lender_ref, me_ref, in_ref, out_ref):
    my_row, my_col = me_ref[0] // per_row, me_ref[0] % per_row
    out_ref[...] = jnp.zeros_like(out_ref)
    for y in range(in_ref.shape[0]):
        target = lender_ref[y * per_row + my_col]

        @pl.when(target // per_row == my_row)
        def _():
            out_ref[target % per_row] = in_ref[y]


def place_back_kernel(per_row, lender_ref, me_ref, in_ref, out_ref):
    my_row, my_col = me_ref[0] // per_row, me_ref[0] % per_row
    for y in range(out_ref.shape[0]):
        source = lender_ref[y * per_row + my_col]
        mine = source // per_row == my_row

        @pl.when(mine)
        def _():
            out_ref[y] = in_ref[source % per_row]

        @pl.when(jnp.logical_not(mine))
        def _():
            out_ref[y] = jnp.zeros(out_ref.shape[1:], BF16)


def merged(in_ref):
    total = in_ref[0].astype(F32)
    for i in range(1, in_ref.shape[0]):
        total = total + in_ref[i].astype(F32)
    return total


def pieces(x, count):
    found = []
    for _ in range(count):
        piece = x.astype(BF16).astype(F32)
        found.append(piece)
        x = x - piece
    return found


def lent_kernel(in_ref, k_ref, v_ref, out_ref):
    message = merged(in_ref)
    q = message[:QROWS].astype(BF16)
    fills = message[QROWS:]
    block_len = k_ref.shape[1]
    k = k_ref[...].reshape(-1, HEAD)
    v = v_ref[...].reshape(-1, HEAD)
    s = dot_t(q, k) * SCALE
    lane = tile_iota(1).astype(F32)
    scores, valid = [], []
    for p in range(k_ref.shape[0]):
        scores.append(s[:, p * block_len : (p + 1) * block_len])
        valid.append(per_head(lane < fills[:, p : p + 1]))
    top, total, weights = soft_part(scores, valid)
    wide = jnp.concatenate([w.astype(BF16) for w in weights], axis=1)
    acc = jnp.dot(wide, v, preferred_element_type=F32)
    acc = acc * jnp.where(total > 0.0, 1.0 / jnp.maximum(total, 1e-30), 0.0)
    side = jnp.zeros((TILE, HEAD), F32)
    for h in range(GROUP):
        span = slice(h * TILE, (h + 1) * TILE)
        values = pieces(top[span], PARTS_M) + pieces(total[span], PARTS_L)
        for i, value in enumerate(values):
            side = jnp.where(tile_iota(1) == h * PER_HEAD + i, value, side)
    reply = jnp.concatenate([acc, side], axis=0).astype(BF16)
    for i in range(out_ref.shape[0]):
        out_ref[i] = reply


def project_kernel(in_ref, o_ref, m_ref, l_ref, w_ref, out_ref):
    reply = merged(in_ref)
    side = reply[QROWS:]
    heads = []
    for h in range(GROUP):
        span = slice(h * TILE, (h + 1) * TILE)
        cols = [side[:, h * PER_HEAD + i : h * PER_HEAD + i + 1] for i in range(PER_HEAD)]
        lent_top = cols[0] + cols[1] + cols[2]
        lent_total = cols[3] + cols[4]
        top = jnp.maximum(m_ref[span], lent_top)
        a = jnp.exp(m_ref[span] - top)
        b = jnp.exp(lent_top - top) * lent_total
        mixed = (a * o_ref[span] + b * reply[span]) / (a * l_ref[span] + b)
        heads.append(mixed.astype(BF16))
    attended = jnp.concatenate(heads, axis=1)
    width = out_ref.shape[2]
    for i in range(out_ref.shape[0]):
        out_ref[i] = jnp.dot(
            attended, w_ref[:, i * width : (i + 1) * width], preferred_element_type=F32
        )


def solution(mesh):
    insts, shards = mesh.shape["inst"], mesh.shape["tp"]
    per_row = 16
    lines = insts // per_row
    along_y = [[y * per_row + c for y in range(lines)] for c in range(per_row)]
    along_row = [[y * per_row + c for c in range(per_row)] for y in range(lines)]

    def exchange(x, groups):
        return lax.all_to_all(x, "inst", 0, 0, axis_index_groups=groups, tiled=True)

    def local(
        queries,
        new_keys,
        new_values,
        res_keys,
        res_values,
        lendable_keys,
        lendable_values,
        ctx_len,
        blocks,
        lender,
        out_proj,
    ):
        me = lax.axis_index("inst").astype(jnp.int32).reshape(1)

        def slots(n):
            return jax.ShapeDtypeStruct((n, MSG, HEAD), BF16)

        pack = functools.partial(pack_kernel, res_keys.shape[1], lendable_keys.shape[1])
        def like(x, space=pltpu.VMEM):
            return space(x.shape, x.dtype)

        def out_like(x):
            return jax.ShapeDtypeStruct(x.shape, x.dtype)

        scratch = [
            like(ctx_len, pltpu.SMEM),
            like(blocks, pltpu.SMEM),
            like(queries),
            pltpu.SemaphoreType.DMA((3,)),
        ]
        sent = call(pack, slots(lines), [HBM] * 3, scratch)(
            *map(off_chip, (ctx_len, blocks, queries))
        )
        held = exchange(sent, along_y)
        part = jax.ShapeDtypeStruct((QROWS, HEAD), F32)
        outs = (part, part, part, *map(out_like, (lendable_keys, lendable_values, lender)))
        given = (queries, new_keys, new_values, res_keys, res_values)
        scratch = [like(ctx_len, pltpu.SMEM), *map(like, given), pltpu.SemaphoreType.DMA((9,))]
        *home, lent_k, lent_v, table = call(home_kernel, outs, [HBM] * 9, scratch)(
            *map(off_chip, (ctx_len, *given, lendable_keys, lendable_values, lender))
        )
        place_out = functools.partial(place_out_kernel, per_row)
        placed = call(place_out, slots(per_row), [SMEM, SMEM, VMEM])(table, me, held)
        arrived = exchange(placed, along_row)
        reply = call(lent_kernel, slots(per_row), [VMEM] * 3)(
            arrived, lent_k, lent_v
        )
        held_back = exchange(reply, along_row)
        place_back = functools.partial(place_back_kernel, per_row)
        placed_back = call(place_back, slots(lines), [SMEM, SMEM, VMEM])(table, me, held_back)
        returned = exchange(placed_back, along_y)
        width = out_proj.shape[1] // shards
        terms = call(
            project_kernel,
            jax.ShapeDtypeStruct((shards, TILE, width), F32),
            [VMEM] * 5,
        )(returned, *home, out_proj)
        shares = lax.all_to_all(terms, "tp", 0, 0, tiled=True)
        return jnp.sum(shares, axis=0).astype(BF16).reshape(ROWS, STEPS, width)

    in_specs = (
        P("inst", None, "tp"),
        P("inst", None, "tp"),
        P("inst", None, "tp"),
        P("inst", None, "tp"),
        P("inst", None, "tp"),
        P("inst", None, "tp"),
        P("inst", None, "tp"),
        P("inst"),
        P("inst", None),
        P(),
        P("tp", None),
    )
    out_specs = P("inst", None, "tp")
    return jax.shard_map(local, mesh=mesh, in_specs=in_specs, out_specs=out_specs, check_vma=False)
```

```python
import functools
import math

import jax
import jax.numpy as jnp
from jax import lax
from jax.experimental import pallas as pl
from jax.experimental.pallas import tpu as pltpu
from jax.sharding import PartitionSpec as P

HEAD = 128
GROUP = 5
ROWS = 2
STEPS = 4
TILE = ROWS * STEPS
QROWS = GROUP * TILE
MSG = 48
OUTBOUND = MSG + QROWS
LOW = -1e30
PARTS_M = 3
PARTS_L = 2
PER_HEAD = PARTS_M + PARTS_L
SIDE_AT = 8
SCALE = 1.0 / math.sqrt(HEAD)
F32 = jnp.float32
BF16 = jnp.bfloat16

VMEM = pl.BlockSpec(memory_space=pltpu.VMEM)
SMEM = pl.BlockSpec(memory_space=pltpu.SMEM)
HBM = pl.BlockSpec(memory_space=pltpu.HBM)


def off_chip(x):
    return pltpu.with_memory_space_constraint(x, pltpu.HBM)


def kept(x):
    return pltpu.with_memory_space_constraint(x, pltpu.VMEM)


def KEPT(x):
    return pltpu.VMEM(x.shape, x.dtype)


def call(kernel, outs, specs, scratch=(), limit=32 * 1024 * 1024):
    return pl.pallas_call(
        kernel,
        out_shape=outs,
        in_specs=specs,
        out_specs=jax.tree.map(lambda _: VMEM, outs),
        scratch_shapes=scratch,
        compiler_params=pltpu.CompilerParams(vmem_limit_bytes=limit),
    )


def head_rows(q_ref):
    q = jnp.concatenate([q_ref[r].astype(F32) for r in range(ROWS)], axis=0)
    return jnp.concatenate([q[:, h * HEAD : (h + 1) * HEAD] for h in range(GROUP)], axis=0)


def fetch(pairs, sems):
    copies = [pltpu.make_async_copy(s, d, sems.at[i]) for i, (s, d) in enumerate(pairs)]
    for copy in copies:
        copy.start()
    return copies


def tile_iota(dim):
    return lax.broadcasted_iota(jnp.int32, (TILE, HEAD), dim)


def per_head(tile):
    return jnp.concatenate([tile] * GROUP, axis=0)


def soft_part(scores, valid):
    masked = [jnp.where(v, s, LOW) for s, v in zip(scores, valid)]
    tops = [jnp.max(s, axis=1, keepdims=True) for s in masked]
    top = functools.reduce(jnp.maximum, tops)
    weights = [jnp.where(v, jnp.exp(s - top), 0.0) for s, v in zip(masked, valid)]
    total = sum(jnp.sum(w, axis=1, keepdims=True) for w in weights)
    return top, total, weights


def dot_t(a, b):
    return lax.dot_general(a, b, (((1,), (1,)), ((), ())), preferred_element_type=F32)


def pieces(x, count):
    found = []
    for _ in range(count):
        piece = x.astype(BF16).astype(F32)
        found.append(piece)
        x = x - piece
    return found


def with_sides(side, top, total):
    for h in range(GROUP):
        span = slice(h * TILE, (h + 1) * TILE)
        values = pieces(top[span], PARTS_M) + pieces(total[span], PARTS_L)
        for i, value in enumerate(values):
            side = jnp.where(tile_iota(1) == SIDE_AT + h * PER_HEAD + i, value, side)
    return side


def sides(side, h):
    first = SIDE_AT + h * PER_HEAD
    cols = [side[:, first + i : first + i + 1] for i in range(PER_HEAD)]
    return cols[0] + cols[1] + cols[2], cols[3] + cols[4]


def home_kernel(
    ctx_hbm,
    blocks_hbm,
    q_hbm,
    nk_hbm,
    nv_hbm,
    k_hbm,
    v_hbm,
    lk_hbm,
    lv_hbm,
    lender_hbm,
    out_ref,
    lk_ref,
    lv_ref,
    lender_ref,
    ctx_ref,
    blocks_ref,
    q_ref,
    nk_ref,
    nv_ref,
    k_ref,
    v_ref,
    sems,
):
    pairs = [
        (q_hbm, q_ref),
        (k_hbm, k_ref),
        (ctx_hbm, ctx_ref),
        (blocks_hbm, blocks_ref),
        (nk_hbm, nk_ref),
        (nv_hbm, nv_ref),
        (v_hbm, v_ref),
        (lender_hbm, lender_ref),
        (lk_hbm, lk_ref),
        (lv_hbm, lv_ref),
    ]
    copies = fetch(pairs, sems)
    for copy in copies[:7]:
        copy.wait()
    rows = head_rows(q_ref)
    q = rows.astype(BF16)
    res_len, block_len = k_ref.shape[1], lk_ref.shape[1]
    request, step, lane = tile_iota(0) // STEPS, tile_iota(0) % STEPS, tile_iota(1)
    side = jnp.zeros((TILE, HEAD), F32)
    for r in range(ROWS):
        for i in range(blocks_ref.shape[1]):
            fill = jnp.clip(ctx_ref[r] - res_len - i * block_len, 0, block_len)
            hit = (request == r) & (lane == blocks_ref[r, i])
            side = jnp.where(hit, fill.astype(F32), side)
    scores, valid = [], []
    for r in range(ROWS):
        s = dot_t(q, k_ref[r]) * SCALE
        for c in range(res_len // HEAD):
            scores.append(s[:, c * HEAD : (c + 1) * HEAD])
            valid.append(per_head((request == r) & (lane + c * HEAD < ctx_ref[r])))
    blank = jnp.zeros((HEAD - TILE, HEAD), F32)

    def fresh(ref):
        return jnp.concatenate([ref[r].astype(F32) for r in range(ROWS)] + [blank], axis=0)

    scores.append(dot_t(q, fresh(nk_ref).astype(BF16)) * SCALE)
    valid.append(
        per_head((lane < TILE) & (lane // STEPS == request) & (lane % STEPS <= step))
    )
    top, total, weights = soft_part(scores, valid)
    w = [x.astype(BF16) for x in weights]
    acc = jnp.dot(w[-1], fresh(nv_ref).astype(BF16), preferred_element_type=F32)
    per = res_len // HEAD
    for r in range(ROWS):
        wide = jnp.concatenate(w[r * per : (r + 1) * per], axis=1)
        acc = acc + jnp.dot(wide, v_ref[r], preferred_element_type=F32)
    side = with_sides(side, top, total)
    message = jnp.concatenate([rows, side, acc / total], axis=0).astype(BF16)
    for i in range(out_ref.shape[0]):
        out_ref[i] = message
    for copy in copies[7:]:
        copy.wait()


def place_kernel(lender_ref, me_ref, in_ref, out_ref):
    per_row = out_ref.shape[0]
    out_ref[...] = jnp.zeros_like(out_ref)
    for y in range(in_ref.shape[0]):
        target = lender_ref[y * per_row + me_ref[1]]

        @pl.when(target // per_row == me_ref[0])
        def _():
            out_ref[target % per_row] = in_ref[y, :MSG]


def merged(in_ref):
    total = in_ref[0].astype(F32)
    for i in range(1, in_ref.shape[0]):
        total = total + in_ref[i].astype(F32)
    return total


def lent_kernel(in_ref, k_ref, v_ref, out_ref):
    message = merged(in_ref)
    q = message[:QROWS].astype(BF16)
    fills = message[QROWS:]
    block_len = k_ref.shape[1]
    k = k_ref[...].reshape(-1, HEAD)
    v = v_ref[...].reshape(-1, HEAD)
    s = dot_t(q, k) * SCALE
    lane = tile_iota(1).astype(F32)
    scores, valid = [], []
    for p in range(k_ref.shape[0]):
        scores.append(s[:, p * block_len : (p + 1) * block_len])
        valid.append(per_head(lane < fills[:, p : p + 1]))
    top, total, weights = soft_part(scores, valid)
    wide = jnp.concatenate([w.astype(BF16) for w in weights], axis=1)
    acc = jnp.dot(wide, v, preferred_element_type=F32)
    acc = acc * jnp.where(total > 0.0, 1.0 / jnp.maximum(total, 1e-30), 0.0)
    side = with_sides(jnp.zeros((TILE, HEAD), F32), top, total)
    reply = jnp.concatenate([acc, side], axis=0).astype(BF16)
    for i in range(out_ref.shape[0]):
        out_ref[i] = reply


def project_kernel(lender_ref, me_ref, held_ref, back_ref, w_ref, out_ref, mixed_ref):
    per_row, lines = back_ref.shape[0], held_ref.shape[0]
    mixed_ref[...] = jnp.zeros_like(mixed_ref)
    for y in range(lines):
        source = lender_ref[y * per_row + me_ref[1]]

        @pl.when(source // per_row == me_ref[0])
        def _():
            home = held_ref[y].astype(F32)
            lent = back_ref[source % per_row].astype(F32)
            for h in range(GROUP):
                home_top, home_total = sides(home[QROWS:MSG], h)
                lent_top, lent_total = sides(lent[QROWS:], h)
                top = jnp.maximum(home_top, lent_top)
                a = jnp.exp(home_top - top) * home_total
                b = jnp.exp(lent_top - top) * lent_total
                at = h * TILE
                part = a * home[MSG + at : MSG + at + TILE] + b * lent[at : at + TILE]
                mixed_ref[y * TILE : (y + 1) * TILE, h * HEAD : (h + 1) * HEAD] = part / (a + b)

    attended = mixed_ref[...].astype(BF16)
    width = out_ref.shape[2]
    shards = out_ref.shape[0] // lines
    for i in range(shards):
        terms = jnp.dot(
            attended, w_ref[:, i * width : (i + 1) * width], preferred_element_type=F32
        )
        for y in range(lines):
            out_ref[y * shards + i] = terms[y * TILE : (y + 1) * TILE].astype(BF16)


def total_kernel(in_ref, out_ref):
    total = merged(in_ref)
    for r in range(ROWS):
        out_ref[r] = total[r * STEPS : (r + 1) * STEPS].astype(BF16)


def solution(mesh):
    insts, shards = mesh.shape["inst"], mesh.shape["tp"]
    per_row = 16
    lines = insts // per_row
    cut = jax.sharding.Mesh(mesh.devices.reshape(lines, per_row, shards), ("line", "row", "tp"))

    def exchange(x, axes):
        return lax.all_to_all(x, axes, 0, 0, tiled=True)

    def local(
        queries,
        new_keys,
        new_values,
        res_keys,
        res_values,
        lendable_keys,
        lendable_values,
        ctx_len,
        blocks,
        lender,
        out_proj,
    ):
        me = jnp.stack([lax.axis_index("line"), lax.axis_index("row")]).astype(jnp.int32)

        def slots(n, rows=MSG, width=HEAD):
            return jax.ShapeDtypeStruct((n, rows, width), BF16)

        def like(x, space=pltpu.VMEM):
            return space(x.shape, x.dtype)

        numbers = (ctx_len, blocks)
        given = (queries, new_keys, new_values, res_keys, res_values)
        brought = (lendable_keys, lendable_values, lender)
        scratch = [
            *(like(x, pltpu.SMEM) for x in numbers),
            *map(like, given),
            pltpu.SemaphoreType.DMA((10,)),
        ]
        outs = (slots(lines, OUTBOUND), *map(KEPT, brought))
        sent, lent_k, lent_v, table = call(home_kernel, outs, [HBM] * 10, scratch)(
            *map(off_chip, (*numbers, *given, *brought))
        )
        held = exchange(sent, "line")
        placed = call(place_kernel, slots(per_row), [SMEM, SMEM, VMEM])(table, me, held)
        arrived = exchange(placed, "row")
        reply = call(lent_kernel, slots(per_row), [VMEM] * 3)(arrived, kept(lent_k), kept(lent_v))
        back = exchange(reply, "row")
        width = out_proj.shape[1] // shards
        rows, columns = lines * TILE, out_proj.shape[0]
        terms = call(
            project_kernel,
            slots(lines * shards, TILE, width),
            [SMEM, SMEM, VMEM, VMEM, VMEM],
            [pltpu.VMEM((rows, columns), F32)],
        )(table, me, held, back, out_proj)
        shares = exchange(terms, ("line", "tp"))
        return call(total_kernel, jax.ShapeDtypeStruct((ROWS, STEPS, width), BF16), [VMEM])(shares)

    by_head = P(("line", "row"), None, "tp")
    in_specs = (
        *[by_head] * 7,
        P(("line", "row")),
        P(("line", "row"), None),
        P(),
        P("tp", None),
    )
    return jax.shard_map(
        local, mesh=cut, in_specs=in_specs, out_specs=by_head, check_vma=False
    )
```

```python
import functools
import math

import jax
import jax.numpy as jnp
from jax import lax
from jax.experimental import pallas as pl
from jax.experimental.pallas import tpu as pltpu
from jax.sharding import PartitionSpec as P

HEAD = 128
GROUP = 5
ROWS = 2
STEPS = 4
TILE = ROWS * STEPS
QROWS = GROUP * TILE
MSG = 48
LOW = -1e30
PARTS_M = 3
PARTS_L = 2
PER_HEAD = PARTS_M + PARTS_L
SCALE = 1.0 / math.sqrt(HEAD)
F32 = jnp.float32
BF16 = jnp.bfloat16

VMEM = pl.BlockSpec(memory_space=pltpu.VMEM)
SMEM = pl.BlockSpec(memory_space=pltpu.SMEM)
HBM = pl.BlockSpec(memory_space=pltpu.HBM)


def off_chip(x):
    return pltpu.with_memory_space_constraint(x, pltpu.HBM)


def call(kernel, outs, specs, scratch=(), limit=32 * 1024 * 1024):
    return pl.pallas_call(
        kernel,
        out_shape=outs,
        in_specs=specs,
        out_specs=jax.tree.map(lambda _: VMEM, outs),
        scratch_shapes=scratch,
        compiler_params=pltpu.CompilerParams(vmem_limit_bytes=limit),
    )


def head_rows(q_ref):
    q = jnp.concatenate([q_ref[r].astype(F32) for r in range(ROWS)], axis=0)
    return jnp.concatenate([q[:, h * HEAD : (h + 1) * HEAD] for h in range(GROUP)], axis=0)


def fetch(pairs, sems):
    copies = [pltpu.make_async_copy(s, d, sems.at[i]) for i, (s, d) in enumerate(pairs)]
    for copy in copies:
        copy.start()
    return copies


def tile_iota(dim):
    return lax.broadcasted_iota(jnp.int32, (TILE, HEAD), dim)


def per_head(tile):
    return jnp.concatenate([tile] * GROUP, axis=0)


def pack_kernel(
    res_len, block_len, ctx_hbm, blocks_hbm, q_hbm, out_ref, ctx_ref, blocks_ref, q_ref, sems
):
    pairs = [(q_hbm, q_ref), (ctx_hbm, ctx_ref), (blocks_hbm, blocks_ref)]
    for copy in fetch(pairs, sems):
        copy.wait()
    rows = head_rows(q_ref)
    side = jnp.zeros((TILE, HEAD), F32)
    request, lane = tile_iota(0) // STEPS, tile_iota(1)
    for r in range(ROWS):
        for i in range(blocks_ref.shape[1]):
            fill = jnp.clip(ctx_ref[r] - res_len - i * block_len, 0, block_len)
            hit = (request == r) & (lane == blocks_ref[r, i])
            side = jnp.where(hit, fill.astype(F32), side)
    message = jnp.concatenate([rows, side], axis=0).astype(BF16)
    for i in range(out_ref.shape[0]):
        out_ref[i] = message


def soft_part(scores, valid):
    masked = [jnp.where(v, s, LOW) for s, v in zip(scores, valid)]
    tops = [jnp.max(s, axis=1, keepdims=True) for s in masked]
    top = functools.reduce(jnp.maximum, tops)
    weights = [jnp.where(v, jnp.exp(s - top), 0.0) for s, v in zip(masked, valid)]
    total = sum(jnp.sum(w, axis=1, keepdims=True) for w in weights)
    return top, total, weights


def dot_t(a, b):
    return lax.dot_general(a, b, (((1,), (1,)), ((), ())), preferred_element_type=F32)


def home_kernel(
    ctx_hbm,
    q_hbm,
    nk_hbm,
    nv_hbm,
    k_hbm,
    v_hbm,
    lender_hbm,
    o_ref,
    m_ref,
    l_ref,
    lender_ref,
    ctx_ref,
    q_ref,
    nk_ref,
    nv_ref,
    k_ref,
    v_ref,
    sems,
):
    pairs = [
        (ctx_hbm, ctx_ref),
        (q_hbm, q_ref),
        (nk_hbm, nk_ref),
        (k_hbm, k_ref),
        (v_hbm, v_ref),
        (nv_hbm, nv_ref),
        (lender_hbm, lender_ref),
    ]
    for copy in fetch(pairs, sems):
        copy.wait()
    q = head_rows(q_ref).astype(BF16)
    res_len = k_ref.shape[1]
    request, step = tile_iota(0) // STEPS, tile_iota(0) % STEPS
    scores, valid = [], []
    for r in range(ROWS):
        s = dot_t(q, k_ref[r]) * SCALE
        for c in range(res_len // HEAD):
            scores.append(s[:, c * HEAD : (c + 1) * HEAD])
            valid.append(per_head((request == r) & (tile_iota(1) + c * HEAD < ctx_ref[r])))
    fill = jnp.zeros((HEAD - TILE, HEAD), F32)

    def fresh(ref):
        return jnp.concatenate([ref[r].astype(F32) for r in range(ROWS)] + [fill], axis=0)

    scores.append(dot_t(q, fresh(nk_ref).astype(BF16)) * SCALE)
    lane = tile_iota(1)
    valid.append(
        per_head((lane < TILE) & (lane // STEPS == request) & (lane % STEPS <= step))
    )
    top, total, weights = soft_part(scores, valid)
    w = [x.astype(BF16) for x in weights]
    acc = jnp.dot(w[-1], fresh(nv_ref).astype(BF16), preferred_element_type=F32)
    per = res_len // HEAD
    for r in range(ROWS):
        wide = jnp.concatenate(w[r * per : (r + 1) * per], axis=1)
        acc = acc + jnp.dot(wide, v_ref[r], preferred_element_type=F32)
    o_ref[...] = acc
    m_ref[...] = jnp.broadcast_to(top, m_ref.shape)
    l_ref[...] = jnp.broadcast_to(total, l_ref.shape)


def position(per_row):
    me = lax.axis_index("inst")
    return me // per_row, me % per_row


def place_out_kernel(lender_ref, in_ref, lk_hbm, lv_hbm, out_ref, lk_ref, lv_ref, sems):
    copies = fetch([(lk_hbm, lk_ref), (lv_hbm, lv_ref)], sems)
    per_row = out_ref.shape[0]
    my_row, my_col = position(per_row)
    out_ref[...] = jnp.zeros_like(out_ref)
    for y in range(in_ref.shape[0]):
        target = lender_ref[y * per_row + my_col]

        @pl.when(target // per_row == my_row)
        def _():
            out_ref[target % per_row] = in_ref[y]

    for copy in copies:
        copy.wait()


def place_back_kernel(lender_ref, in_ref, out_ref):
    per_row = in_ref.shape[0]
    my_row, my_col = position(per_row)
    out_ref[...] = jnp.zeros_like(out_ref)
    for y in range(out_ref.shape[0]):
        source = lender_ref[y * per_row + my_col]

        @pl.when(source // per_row == my_row)
        def _():
            out_ref[y] = in_ref[source % per_row]


def merged(in_ref):
    total = in_ref[0].astype(F32)
    for i in range(1, in_ref.shape[0]):
        total = total + in_ref[i].astype(F32)
    return total


def pieces(x, count):
    found = []
    for _ in range(count):
        piece = x.astype(BF16).astype(F32)
        found.append(piece)
        x = x - piece
    return found


def lent_kernel(in_ref, k_ref, v_ref, out_ref):
    message = merged(in_ref)
    q = message[:QROWS].astype(BF16)
    fills = message[QROWS:]
    block_len = k_ref.shape[1]
    k = k_ref[...].reshape(-1, HEAD)
    v = v_ref[...].reshape(-1, HEAD)
    s = dot_t(q, k) * SCALE
    lane = tile_iota(1).astype(F32)
    scores, valid = [], []
    for p in range(k_ref.shape[0]):
        scores.append(s[:, p * block_len : (p + 1) * block_len])
        valid.append(per_head(lane < fills[:, p : p + 1]))
    top, total, weights = soft_part(scores, valid)
    wide = jnp.concatenate([w.astype(BF16) for w in weights], axis=1)
    acc = jnp.dot(wide, v, preferred_element_type=F32)
    acc = acc * jnp.where(total > 0.0, 1.0 / jnp.maximum(total, 1e-30), 0.0)
    side = jnp.zeros((TILE, HEAD), F32)
    for h in range(GROUP):
        span = slice(h * TILE, (h + 1) * TILE)
        values = pieces(top[span], PARTS_M) + pieces(total[span], PARTS_L)
        for i, value in enumerate(values):
            side = jnp.where(tile_iota(1) == h * PER_HEAD + i, value, side)
    reply = jnp.concatenate([acc, side], axis=0).astype(BF16)
    for i in range(out_ref.shape[0]):
        out_ref[i] = reply


def project_kernel(in_ref, o_ref, m_ref, l_ref, w_ref, out_ref):
    reply = merged(in_ref)
    side = reply[QROWS:]
    heads = []
    for h in range(GROUP):
        span = slice(h * TILE, (h + 1) * TILE)
        cols = [side[:, h * PER_HEAD + i : h * PER_HEAD + i + 1] for i in range(PER_HEAD)]
        lent_top = cols[0] + cols[1] + cols[2]
        lent_total = cols[3] + cols[4]
        top = jnp.maximum(m_ref[span], lent_top)
        a = jnp.exp(m_ref[span] - top)
        b = jnp.exp(lent_top - top) * lent_total
        mixed = (a * o_ref[span] + b * reply[span]) / (a * l_ref[span] + b)
        heads.append(mixed.astype(BF16))
    attended = jnp.concatenate(heads, axis=1)
    width = out_ref.shape[2]
    for i in range(out_ref.shape[0]):
        out_ref[i] = jnp.dot(
            attended, w_ref[:, i * width : (i + 1) * width], preferred_element_type=F32
        )


def solution(mesh):
    insts, shards = mesh.shape["inst"], mesh.shape["tp"]
    per_row = 16
    lines = insts // per_row
    along_y = [[y * per_row + c for y in range(lines)] for c in range(per_row)]
    along_row = [[y * per_row + c for c in range(per_row)] for y in range(lines)]

    def exchange(x, groups):
        return lax.all_to_all(x, "inst", 0, 0, axis_index_groups=groups, tiled=True)

    def local(
        queries,
        new_keys,
        new_values,
        res_keys,
        res_values,
        lendable_keys,
        lendable_values,
        ctx_len,
        blocks,
        lender,
        out_proj,
    ):
        def slots(n):
            return jax.ShapeDtypeStruct((n, MSG, HEAD), BF16)

        pack = functools.partial(pack_kernel, res_keys.shape[1], lendable_keys.shape[1])
        def like(x, space=pltpu.VMEM):
            return space(x.shape, x.dtype)

        def out_like(x):
            return jax.ShapeDtypeStruct(x.shape, x.dtype)

        scratch = [
            like(ctx_len, pltpu.SMEM),
            like(blocks, pltpu.SMEM),
            like(queries),
            pltpu.SemaphoreType.DMA((3,)),
        ]
        sent = call(pack, slots(lines), [HBM] * 3, scratch)(
            *map(off_chip, (ctx_len, blocks, queries))
        )
        held = exchange(sent, along_y)
        part = jax.ShapeDtypeStruct((QROWS, HEAD), F32)
        outs = (part, part, part, out_like(lender))
        given = (queries, new_keys, new_values, res_keys, res_values)
        scratch = [like(ctx_len, pltpu.SMEM), *map(like, given), pltpu.SemaphoreType.DMA((7,))]
        *home, table = call(home_kernel, outs, [HBM] * 7, scratch)(
            *map(off_chip, (ctx_len, *given, lender))
        )
        outs = (slots(per_row), out_like(lendable_keys), out_like(lendable_values))
        placed, lent_k, lent_v = call(
            place_out_kernel, outs, [SMEM, VMEM, HBM, HBM], [pltpu.SemaphoreType.DMA((2,))]
        )(table, held, off_chip(lendable_keys), off_chip(lendable_values))
        arrived = exchange(placed, along_row)
        reply = call(lent_kernel, slots(per_row), [VMEM] * 3)(
            arrived, lent_k, lent_v
        )
        held_back = exchange(reply, along_row)
        placed_back = call(place_back_kernel, slots(lines), [SMEM, VMEM])(table, held_back)
        returned = exchange(placed_back, along_y)
        width = out_proj.shape[1] // shards
        terms = call(
            project_kernel,
            jax.ShapeDtypeStruct((shards, TILE, width), F32),
            [VMEM] * 5,
        )(returned, *home, out_proj)
        shares = lax.all_to_all(terms, "tp", 0, 0, tiled=True)
        return jnp.sum(shares, axis=0).astype(BF16).reshape(ROWS, STEPS, width)

    in_specs = (
        P("inst", None, "tp"),
        P("inst", None, "tp"),
        P("inst", None, "tp"),
        P("inst", None, "tp"),
        P("inst", None, "tp"),
        P("inst", None, "tp"),
        P("inst", None, "tp"),
        P("inst"),
        P("inst", None),
        P(),
        P("tp", None),
    )
    out_specs = P("inst", None, "tp")
    return jax.shard_map(local, mesh=mesh, in_specs=in_specs, out_specs=out_specs, check_vma=False)
```

```python
import functools
import math

import jax
import jax.numpy as jnp
from jax import lax
from jax.experimental import pallas as pl
from jax.experimental.pallas import tpu as pltpu
from jax.sharding import PartitionSpec as P

HEAD = 128
GROUP = 5
ROWS = 2
STEPS = 4
TILE = ROWS * STEPS
QROWS = GROUP * TILE
MSG = 48
LOW = -1e30
PARTS_M = 3
PARTS_L = 2
PER_HEAD = PARTS_M + PARTS_L
SCALE = 1.0 / math.sqrt(HEAD)
F32 = jnp.float32
BF16 = jnp.bfloat16

VMEM = pl.BlockSpec(memory_space=pltpu.VMEM)
HBM = pl.BlockSpec(memory_space=pltpu.HBM)


def off_chip(x):
    return pltpu.with_memory_space_constraint(x, pltpu.HBM)


def call(kernel, outs, specs, scratch=(), limit=32 * 1024 * 1024):
    return pl.pallas_call(
        kernel,
        out_shape=outs,
        in_specs=specs,
        out_specs=jax.tree.map(lambda _: VMEM, outs),
        scratch_shapes=scratch,
        compiler_params=pltpu.CompilerParams(vmem_limit_bytes=limit),
    )


def head_rows(q_ref):
    q = jnp.concatenate([q_ref[r].astype(F32) for r in range(ROWS)], axis=0)
    return jnp.concatenate([q[:, h * HEAD : (h + 1) * HEAD] for h in range(GROUP)], axis=0)


def fetch(pairs, sems):
    copies = [pltpu.make_async_copy(s, d, sems.at[i]) for i, (s, d) in enumerate(pairs)]
    for copy in copies:
        copy.start()
    return copies


def tile_iota(dim):
    return lax.broadcasted_iota(jnp.int32, (TILE, HEAD), dim)


def per_head(tile):
    return jnp.concatenate([tile] * GROUP, axis=0)


def soft_part(scores, valid):
    masked = [jnp.where(v, s, LOW) for s, v in zip(scores, valid)]
    tops = [jnp.max(s, axis=1, keepdims=True) for s in masked]
    top = functools.reduce(jnp.maximum, tops)
    weights = [jnp.where(v, jnp.exp(s - top), 0.0) for s, v in zip(masked, valid)]
    total = sum(jnp.sum(w, axis=1, keepdims=True) for w in weights)
    return top, total, weights


def dot_t(a, b):
    return lax.dot_general(a, b, (((1,), (1,)), ((), ())), preferred_element_type=F32)


def first_kernel(
    ctx_hbm,
    blocks_hbm,
    lender_hbm,
    q_hbm,
    nk_hbm,
    nv_hbm,
    k_hbm,
    v_hbm,
    lk_hbm,
    lv_hbm,
    out_ref,
    o_ref,
    m_ref,
    l_ref,
    pick_ref,
    lk_ref,
    lv_ref,
    ctx_ref,
    blocks_ref,
    lender_ref,
    q_ref,
    nk_ref,
    nv_ref,
    k_ref,
    v_ref,
    sems,
):
    pairs = [
        (q_hbm, q_ref),
        (k_hbm, k_ref),
        (lender_hbm, lender_ref),
        (ctx_hbm, ctx_ref),
        (blocks_hbm, blocks_ref),
        (nk_hbm, nk_ref),
        (v_hbm, v_ref),
        (nv_hbm, nv_ref),
        (lk_hbm, lk_ref),
        (lv_hbm, lv_ref),
    ]
    copies = fetch(pairs, sems)
    request, step, lane = tile_iota(0) // STEPS, tile_iota(0) % STEPS, tile_iota(1)

    copies[2].wait()
    lines = out_ref.shape[0]
    per_row = pick_ref.shape[0] // lines
    me = lax.axis_index("inst")
    row, col = me // per_row, me % per_row
    target = jnp.zeros((lines, HEAD), jnp.int32)
    for y in range(lines):
        here = lax.broadcasted_iota(jnp.int32, (lines, HEAD), 0) == y
        target = jnp.where(here, lender_ref[y * per_row + col] - row * per_row, target)
    for s in range(per_row):
        pick_ref[s * lines : (s + 1) * lines] = jnp.where(target == s, 1.0, 0.0)

    for copy in [copies[0], *copies[3:5]]:
        copy.wait()
    rows = head_rows(q_ref)
    q = rows.astype(BF16)
    res_len, block_len = k_ref.shape[1], lk_ref.shape[1]
    side = jnp.zeros((TILE, HEAD), F32)
    for r in range(ROWS):
        for i in range(blocks_ref.shape[1]):
            fill = jnp.clip(ctx_ref[r] - res_len - i * block_len, 0, block_len)
            hit = (request == r) & (lane == blocks_ref[r, i])
            side = jnp.where(hit, fill.astype(F32), side)
    message = jnp.concatenate([rows, side], axis=0).astype(BF16)
    for i in range(lines):
        out_ref[i] = message

    for copy in [copies[1], copies[5]]:
        copy.wait()
    scores, valid = [], []
    for r in range(ROWS):
        s = dot_t(q, k_ref[r]) * SCALE
        for c in range(res_len // HEAD):
            scores.append(s[:, c * HEAD : (c + 1) * HEAD])
            valid.append(per_head((request == r) & (lane + c * HEAD < ctx_ref[r])))
    blank = jnp.zeros((HEAD - TILE, HEAD), F32)

    def fresh(ref):
        return jnp.concatenate([ref[r].astype(F32) for r in range(ROWS)] + [blank], axis=0)

    scores.append(dot_t(q, fresh(nk_ref).astype(BF16)) * SCALE)
    valid.append(
        per_head((lane < TILE) & (lane // STEPS == request) & (lane % STEPS <= step))
    )
    top, total, weights = soft_part(scores, valid)
    for copy in copies[6:8]:
        copy.wait()
    w = [x.astype(BF16) for x in weights]
    acc = jnp.dot(w[-1], fresh(nv_ref).astype(BF16), preferred_element_type=F32)
    per = res_len // HEAD
    for r in range(ROWS):
        wide = jnp.concatenate(w[r * per : (r + 1) * per], axis=1)
        acc = acc + jnp.dot(wide, v_ref[r], preferred_element_type=F32)
    o_ref[...] = acc
    m_ref[...] = jnp.broadcast_to(top, m_ref.shape)
    l_ref[...] = jnp.broadcast_to(total, l_ref.shape)
    for copy in copies[8:]:
        copy.wait()


def place(pick_ref, in_ref, out_ref, place_of):
    held = [in_ref[i].astype(F32) for i in range(in_ref.shape[0])]
    for o in range(out_ref.shape[0]):
        tiles = [jnp.zeros((TILE, HEAD), F32)] * (MSG // TILE)
        for i, message in enumerate(held):
            at = place_of(i, o)
            mine = jnp.broadcast_to(pick_ref[at : at + 1], (TILE, HEAD)) > 0.5
            tiles = [
                jnp.where(mine, message[t * TILE : (t + 1) * TILE], tile)
                for t, tile in enumerate(tiles)
            ]
        out_ref[o] = jnp.concatenate(tiles, axis=0).astype(BF16)


def place_out_kernel(pick_ref, in_ref, out_ref):
    place(pick_ref, in_ref, out_ref, lambda y, s: s * in_ref.shape[0] + y)


def place_back_kernel(pick_ref, in_ref, out_ref):
    place(pick_ref, in_ref, out_ref, lambda s, y: s * out_ref.shape[0] + y)


def merged(in_ref):
    total = in_ref[0].astype(F32)
    for i in range(1, in_ref.shape[0]):
        total = total + in_ref[i].astype(F32)
    return total


def pieces(x, count):
    found = []
    for _ in range(count):
        piece = x.astype(BF16).astype(F32)
        found.append(piece)
        x = x - piece
    return found


def lent_kernel(in_ref, k_ref, v_ref, out_ref):
    message = merged(in_ref)
    q = message[:QROWS].astype(BF16)
    fills = message[QROWS:]
    block_len = k_ref.shape[1]
    k = k_ref[...].reshape(-1, HEAD)
    v = v_ref[...].reshape(-1, HEAD)
    s = dot_t(q, k) * SCALE
    lane = tile_iota(1).astype(F32)
    scores, valid = [], []
    for p in range(k_ref.shape[0]):
        scores.append(s[:, p * block_len : (p + 1) * block_len])
        valid.append(per_head(lane < fills[:, p : p + 1]))
    top, total, weights = soft_part(scores, valid)
    wide = jnp.concatenate([w.astype(BF16) for w in weights], axis=1)
    acc = jnp.dot(wide, v, preferred_element_type=F32)
    acc = acc * jnp.where(total > 0.0, 1.0 / jnp.maximum(total, 1e-30), 0.0)
    side = jnp.zeros((TILE, HEAD), F32)
    for h in range(GROUP):
        span = slice(h * TILE, (h + 1) * TILE)
        values = pieces(top[span], PARTS_M) + pieces(total[span], PARTS_L)
        for i, value in enumerate(values):
            side = jnp.where(tile_iota(1) == h * PER_HEAD + i, value, side)
    reply = jnp.concatenate([acc, side], axis=0).astype(BF16)
    for i in range(out_ref.shape[0]):
        out_ref[i] = reply


def project_kernel(in_ref, o_ref, m_ref, l_ref, w_ref, out_ref):
    reply = merged(in_ref)
    side = reply[QROWS:]
    heads = []
    for h in range(GROUP):
        span = slice(h * TILE, (h + 1) * TILE)
        cols = [side[:, h * PER_HEAD + i : h * PER_HEAD + i + 1] for i in range(PER_HEAD)]
        lent_top = cols[0] + cols[1] + cols[2]
        lent_total = cols[3] + cols[4]
        top = jnp.maximum(m_ref[span], lent_top)
        a = jnp.exp(m_ref[span] - top)
        b = jnp.exp(lent_top - top) * lent_total
        mixed = (a * o_ref[span] + b * reply[span]) / (a * l_ref[span] + b)
        heads.append(mixed.astype(BF16))
    attended = jnp.concatenate(heads, axis=1)
    width = out_ref.shape[2]
    for i in range(out_ref.shape[0]):
        out_ref[i] = jnp.dot(
            attended, w_ref[:, i * width : (i + 1) * width], preferred_element_type=F32
        )


def solution(mesh):
    insts, shards = mesh.shape["inst"], mesh.shape["tp"]
    per_row = 16
    lines = insts // per_row
    along_y = [[y * per_row + c for y in range(lines)] for c in range(per_row)]
    along_row = [[y * per_row + c for c in range(per_row)] for y in range(lines)]

    def exchange(x, groups):
        return lax.all_to_all(x, "inst", 0, 0, axis_index_groups=groups, tiled=True)

    def local(
        queries,
        new_keys,
        new_values,
        res_keys,
        res_values,
        lendable_keys,
        lendable_values,
        ctx_len,
        blocks,
        lender,
        out_proj,
    ):
        def slots(n):
            return jax.ShapeDtypeStruct((n, MSG, HEAD), BF16)

        def like(x, space=pltpu.VMEM):
            return space(x.shape, x.dtype)

        def out_like(x):
            return jax.ShapeDtypeStruct(x.shape, x.dtype)

        numbers = (ctx_len, blocks, lender)
        given = (queries, new_keys, new_values, res_keys, res_values)
        lent = (lendable_keys, lendable_values)
        part = jax.ShapeDtypeStruct((QROWS, HEAD), F32)
        picks = jax.ShapeDtypeStruct((insts, HEAD), F32)
        outs = (slots(lines), part, part, part, picks, *map(out_like, lent))
        scratch = [
            *(like(x, pltpu.SMEM) for x in numbers),
            *map(like, given),
            pltpu.SemaphoreType.DMA((10,)),
        ]
        sent, *home, picked, lent_k, lent_v = call(first_kernel, outs, [HBM] * 10, scratch)(
            *map(off_chip, (*numbers, *given, *lent))
        )
        held = exchange(sent, along_y)
        placed = call(place_out_kernel, slots(per_row), [VMEM] * 2)(picked, held)
        arrived = exchange(placed, along_row)
        reply = call(lent_kernel, slots(per_row), [VMEM] * 3)(
            arrived, lent_k, lent_v
        )
        held_back = exchange(reply, along_row)
        placed_back = call(place_back_kernel, slots(lines), [VMEM] * 2)(picked, held_back)
        returned = exchange(placed_back, along_y)
        width = out_proj.shape[1] // shards
        terms = call(
            project_kernel,
            jax.ShapeDtypeStruct((shards, TILE, width), F32),
            [VMEM] * 5,
        )(returned, *home, out_proj)
        shares = lax.all_to_all(terms, "tp", 0, 0, tiled=True)
        return jnp.sum(shares, axis=0).astype(BF16).reshape(ROWS, STEPS, width)

    in_specs = (
        P("inst", None, "tp"),
        P("inst", None, "tp"),
        P("inst", None, "tp"),
        P("inst", None, "tp"),
        P("inst", None, "tp"),
        P("inst", None, "tp"),
        P("inst", None, "tp"),
        P("inst"),
        P("inst", None),
        P(),
        P("tp", None),
    )
    out_specs = P("inst", None, "tp")
    return jax.shard_map(local, mesh=mesh, in_specs=in_specs, out_specs=out_specs, check_vma=False)
```

```python
import functools
import math

import jax
import jax.numpy as jnp
from jax import lax
from jax.experimental import pallas as pl
from jax.experimental.pallas import tpu as pltpu
from jax.sharding import PartitionSpec as P

HEAD = 128
GROUP = 5
ROWS = 2
STEPS = 4
TILE = ROWS * STEPS
QROWS = GROUP * TILE
PARTS = GROUP * ROWS + 1
MSG = PARTS * HEAD
LOW = -1e30
PARTS_M = 3
PARTS_L = 2
PIECES = PARTS_M + PARTS_L
SCALE = 1.0 / math.sqrt(HEAD)
F32 = jnp.float32
BF16 = jnp.bfloat16

VMEM = pl.BlockSpec(memory_space=pltpu.VMEM)
HBM = pl.BlockSpec(memory_space=pltpu.HBM)


def off_chip(x):
    return pltpu.with_memory_space_constraint(x, pltpu.HBM)


def call(kernel, outs, specs, scratch=(), limit=32 * 1024 * 1024):
    return pl.pallas_call(
        kernel,
        out_shape=outs,
        in_specs=specs,
        out_specs=jax.tree.map(lambda _: VMEM, outs),
        scratch_shapes=scratch,
        compiler_params=pltpu.CompilerParams(vmem_limit_bytes=limit),
    )


def head_rows(q_ref):
    q = jnp.concatenate([q_ref[r].astype(F32) for r in range(ROWS)], axis=0)
    return jnp.concatenate([q[:, h * HEAD : (h + 1) * HEAD] for h in range(GROUP)], axis=0)


def fetch(pairs, sems):
    copies = [pltpu.make_async_copy(s, d, sems.at[i]) for i, (s, d) in enumerate(pairs)]
    for copy in copies:
        copy.start()
    return copies


def tile_iota(dim):
    return lax.broadcasted_iota(jnp.int32, (TILE, HEAD), dim)


def upper():
    return tile_iota(0) >= STEPS


def by_request(side, apart):
    both = jnp.concatenate([side] * ROWS, axis=0)
    return jnp.where(upper(), pltpu.roll(both, HEAD - apart, axis=1), both)


def joined(message, h):
    at = h * ROWS * HEAD
    return jnp.concatenate(
        [message[:, at + r * HEAD : at + (r + 1) * HEAD] for r in range(ROWS)], axis=0
    )


def per_head(tile):
    return jnp.concatenate([tile] * GROUP, axis=0)


def soft_part(scores, valid):
    masked = [jnp.where(v, s, LOW) for s, v in zip(scores, valid)]
    tops = [jnp.max(s, axis=1, keepdims=True) for s in masked]
    top = functools.reduce(jnp.maximum, tops)
    weights = [jnp.where(v, jnp.exp(s - top), 0.0) for s, v in zip(masked, valid)]
    total = sum(jnp.sum(w, axis=1, keepdims=True) for w in weights)
    return top, total, weights


def dot_t(a, b):
    return lax.dot_general(a, b, (((1,), (1,)), ((), ())), preferred_element_type=F32)


def first_kernel(
    ctx_hbm,
    blocks_hbm,
    lender_hbm,
    q_hbm,
    nk_hbm,
    nv_hbm,
    k_hbm,
    v_hbm,
    lk_hbm,
    lv_hbm,
    out_ref,
    o_ref,
    m_ref,
    l_ref,
    pick_ref,
    lk_ref,
    lv_ref,
    ctx_ref,
    blocks_ref,
    lender_ref,
    q_ref,
    nk_ref,
    nv_ref,
    k_ref,
    v_ref,
    sems,
):
    pairs = [
        (q_hbm, q_ref),
        (k_hbm, k_ref),
        (lender_hbm, lender_ref),
        (ctx_hbm, ctx_ref),
        (blocks_hbm, blocks_ref),
        (nk_hbm, nk_ref),
        (v_hbm, v_ref),
        (nv_hbm, nv_ref),
        (lk_hbm, lk_ref),
        (lv_hbm, lv_ref),
    ]
    copies = fetch(pairs, sems)
    request, step, lane = tile_iota(0) // STEPS, tile_iota(0) % STEPS, tile_iota(1)

    copies[2].wait()
    lines = out_ref.shape[0]
    per_row = pick_ref.shape[0] // lines
    me = lax.axis_index("inst")
    row, col = me // per_row, me % per_row
    target = jnp.zeros((lines, HEAD), jnp.int32)
    for y in range(lines):
        here = lax.broadcasted_iota(jnp.int32, (lines, HEAD), 0) == y
        target = jnp.where(here, lender_ref[y * per_row + col] - row * per_row, target)
    for s in range(per_row):
        pick_ref[s * lines : (s + 1) * lines] = jnp.where(target == s, 1.0, 0.0)

    for copy in [copies[0], *copies[3:5]]:
        copy.wait()
    q = head_rows(q_ref).astype(BF16)
    res_len, block_len = k_ref.shape[1], lk_ref.shape[1]
    side = jnp.zeros((STEPS, HEAD), F32)
    for r in range(ROWS):
        for i in range(blocks_ref.shape[1]):
            fill = jnp.clip(ctx_ref[r] - res_len - i * block_len, 0, block_len)
            hit = lane[:STEPS] == r * lk_ref.shape[0] + blocks_ref[r, i]
            side = jnp.where(hit, fill.astype(F32), side)
    steps = [q_ref[r].astype(F32) for r in range(ROWS)]
    tiles = [steps[r][:, h * HEAD : (h + 1) * HEAD] for h in range(GROUP) for r in range(ROWS)]
    message = jnp.concatenate([*tiles, side], axis=1).astype(BF16)
    for i in range(lines):
        out_ref[i] = message

    for copy in [copies[1], copies[5]]:
        copy.wait()
    scores, valid = [], []
    for r in range(ROWS):
        s = dot_t(q, k_ref[r]) * SCALE
        for c in range(res_len // HEAD):
            scores.append(s[:, c * HEAD : (c + 1) * HEAD])
            valid.append(per_head((request == r) & (lane + c * HEAD < ctx_ref[r])))
    blank = jnp.zeros((HEAD - TILE, HEAD), F32)

    def fresh(ref):
        return jnp.concatenate([ref[r].astype(F32) for r in range(ROWS)] + [blank], axis=0)

    scores.append(dot_t(q, fresh(nk_ref).astype(BF16)) * SCALE)
    valid.append(
        per_head((lane < TILE) & (lane // STEPS == request) & (lane % STEPS <= step))
    )
    top, total, weights = soft_part(scores, valid)
    for copy in copies[6:8]:
        copy.wait()
    w = [x.astype(BF16) for x in weights]
    acc = jnp.dot(w[-1], fresh(nv_ref).astype(BF16), preferred_element_type=F32)
    per = res_len // HEAD
    for r in range(ROWS):
        wide = jnp.concatenate(w[r * per : (r + 1) * per], axis=1)
        acc = acc + jnp.dot(wide, v_ref[r], preferred_element_type=F32)
    o_ref[...] = acc
    m_ref[...] = jnp.broadcast_to(top, m_ref.shape)
    l_ref[...] = jnp.broadcast_to(total, l_ref.shape)
    for copy in copies[8:]:
        copy.wait()


def place(pick_ref, in_ref, out_ref, place_of):
    held = []
    for i in range(in_ref.shape[0]):
        message = in_ref[i].astype(F32)
        side = jnp.concatenate([message[:, MSG - HEAD :]] * ROWS, axis=0)
        held.append([*(joined(message, h) for h in range(GROUP)), side])
    for o in range(out_ref.shape[0]):
        tiles = [jnp.zeros((TILE, HEAD), F32)] * (GROUP + 1)
        for i, message in enumerate(held):
            at = place_of(i, o)
            mine = jnp.broadcast_to(pick_ref[at : at + 1], (TILE, HEAD)) > 0.5
            tiles = [jnp.where(mine, m, tile) for m, tile in zip(message, tiles)]
        halves = [t[r * STEPS : (r + 1) * STEPS] for t in tiles[:GROUP] for r in range(ROWS)]
        out_ref[o] = jnp.concatenate([*halves, tiles[GROUP][:STEPS]], axis=1).astype(BF16)


def place_out_kernel(pick_ref, in_ref, out_ref):
    place(pick_ref, in_ref, out_ref, lambda y, s: s * in_ref.shape[0] + y)


def place_back_kernel(pick_ref, in_ref, out_ref):
    place(pick_ref, in_ref, out_ref, lambda s, y: s * out_ref.shape[0] + y)


def merged(in_ref):
    total = in_ref[0].astype(F32)
    for i in range(1, in_ref.shape[0]):
        total = total + in_ref[i].astype(F32)
    return total


def pieces(x, count):
    found = []
    for _ in range(count):
        piece = x.astype(BF16).astype(F32)
        found.append(piece)
        x = x - piece
    return found


def lent_kernel(in_ref, k_ref, v_ref, out_ref):
    message = merged(in_ref)
    q = jnp.concatenate([joined(message, h) for h in range(GROUP)], axis=0).astype(BF16)
    fills = by_request(message[:, MSG - HEAD :], k_ref.shape[0])
    block_len = k_ref.shape[1]
    k = k_ref[...].reshape(-1, HEAD)
    v = v_ref[...].reshape(-1, HEAD)
    s = dot_t(q, k) * SCALE
    lane = tile_iota(1).astype(F32)
    scores, valid = [], []
    for p in range(k_ref.shape[0]):
        scores.append(s[:, p * block_len : (p + 1) * block_len])
        valid.append(per_head(lane < fills[:, p : p + 1]))
    top, total, weights = soft_part(scores, valid)
    wide = jnp.concatenate([w.astype(BF16) for w in weights], axis=1)
    acc = jnp.dot(wide, v, preferred_element_type=F32)
    acc = acc * jnp.where(total > 0.0, 1.0 / jnp.maximum(total, 1e-30), 0.0)
    side = jnp.zeros((TILE, HEAD), F32)
    for h in range(GROUP):
        span = slice(h * TILE, (h + 1) * TILE)
        values = pieces(top[span], PARTS_M) + pieces(total[span], PARTS_L)
        for i, value in enumerate(values):
            side = jnp.where(tile_iota(1) == h * ROWS * PIECES + i, value, side)
    side = side[:STEPS] + pltpu.roll(side, PIECES, axis=1)[STEPS:]
    tiles = [acc[i * STEPS : (i + 1) * STEPS] for i in range(GROUP * ROWS)]
    reply = jnp.concatenate([*tiles, side], axis=1).astype(BF16)
    for i in range(out_ref.shape[0]):
        out_ref[i] = reply


def project_kernel(in_ref, o_ref, m_ref, l_ref, w_ref, out_ref):
    reply = merged(in_ref)
    side = by_request(reply[:, MSG - HEAD :], PIECES)
    heads = []
    for h in range(GROUP):
        span = slice(h * TILE, (h + 1) * TILE)
        first = h * ROWS * PIECES
        cols = [side[:, first + i : first + i + 1] for i in range(PIECES)]
        lent_top = cols[0] + cols[1] + cols[2]
        lent_total = cols[3] + cols[4]
        top = jnp.maximum(m_ref[span], lent_top)
        a = jnp.exp(m_ref[span] - top)
        b = jnp.exp(lent_top - top) * lent_total
        mixed = (a * o_ref[span] + b * joined(reply, h)) / (a * l_ref[span] + b)
        heads.append(mixed.astype(BF16))
    attended = jnp.concatenate(heads, axis=1)
    width = out_ref.shape[2]
    for i in range(out_ref.shape[0]):
        out_ref[i] = jnp.dot(
            attended, w_ref[:, i * width : (i + 1) * width], preferred_element_type=F32
        )


def solution(mesh):
    insts, shards = mesh.shape["inst"], mesh.shape["tp"]
    per_row = 16
    lines = insts // per_row
    along_y = [[y * per_row + c for y in range(lines)] for c in range(per_row)]
    along_row = [[y * per_row + c for c in range(per_row)] for y in range(lines)]

    def exchange(x, groups):
        return lax.all_to_all(x, "inst", 0, 0, axis_index_groups=groups, tiled=True)

    def local(
        queries,
        new_keys,
        new_values,
        res_keys,
        res_values,
        lendable_keys,
        lendable_values,
        ctx_len,
        blocks,
        lender,
        out_proj,
    ):
        def slots(n):
            return jax.ShapeDtypeStruct((n, STEPS, MSG), BF16)

        def like(x, space=pltpu.VMEM):
            return space(x.shape, x.dtype)

        def out_like(x):
            return jax.ShapeDtypeStruct(x.shape, x.dtype)

        numbers = (ctx_len, blocks, lender)
        given = (queries, new_keys, new_values, res_keys, res_values)
        lent = (lendable_keys, lendable_values)
        part = jax.ShapeDtypeStruct((QROWS, HEAD), F32)
        picks = jax.ShapeDtypeStruct((insts, HEAD), F32)
        outs = (slots(lines), part, part, part, picks, *map(out_like, lent))
        scratch = [
            *(like(x, pltpu.SMEM) for x in numbers),
            *map(like, given),
            pltpu.SemaphoreType.DMA((10,)),
        ]
        sent, *home, picked, lent_k, lent_v = call(first_kernel, outs, [HBM] * 10, scratch)(
            *map(off_chip, (*numbers, *given, *lent))
        )
        held = exchange(sent, along_y)
        placed = call(place_out_kernel, slots(per_row), [VMEM] * 2)(picked, held)
        arrived = exchange(placed, along_row)
        reply = call(lent_kernel, slots(per_row), [VMEM] * 3)(
            arrived, lent_k, lent_v
        )
        held_back = exchange(reply, along_row)
        placed_back = call(place_back_kernel, slots(lines), [VMEM] * 2)(picked, held_back)
        returned = exchange(placed_back, along_y)
        width = out_proj.shape[1] // shards
        terms = call(
            project_kernel,
            jax.ShapeDtypeStruct((shards, TILE, width), F32),
            [VMEM] * 5,
        )(returned, *home, out_proj)
        shares = lax.all_to_all(terms, "tp", 0, 0, tiled=True)
        return jnp.sum(shares, axis=0).astype(BF16).reshape(ROWS, STEPS, width)

    in_specs = (
        P("inst", None, "tp"),
        P("inst", None, "tp"),
        P("inst", None, "tp"),
        P("inst", None, "tp"),
        P("inst", None, "tp"),
        P("inst", None, "tp"),
        P("inst", None, "tp"),
        P("inst"),
        P("inst", None),
        P(),
        P("tp", None),
    )
    out_specs = P("inst", None, "tp")
    return jax.shard_map(local, mesh=mesh, in_specs=in_specs, out_specs=out_specs, check_vma=False)
```

```python
import functools
import math

import jax
import jax.numpy as jnp
from jax import lax
from jax.experimental import pallas as pl
from jax.experimental.pallas import tpu as pltpu
from jax.sharding import PartitionSpec as P

HEAD = 128
GROUP = 5
ROWS = 2
STEPS = 4
TILE = ROWS * STEPS
QROWS = GROUP * TILE
PARTS = GROUP * ROWS + 1
MSG = PARTS * HEAD
LOW = -1e30
PARTS_M = 3
PARTS_L = 2
PIECES = PARTS_M + PARTS_L
SCALE = 1.0 / math.sqrt(HEAD)
LINE = (0, 4, 2, 6, 1, 5, 3, 7)
ROW = (*range(0, 16, 2), *range(1, 16, 2))
SHARD = (0, 2, 1, 3)
F32 = jnp.float32
BF16 = jnp.bfloat16

VMEM = pl.BlockSpec(memory_space=pltpu.VMEM)
HBM = pl.BlockSpec(memory_space=pltpu.HBM)


def off_chip(x):
    return pltpu.with_memory_space_constraint(x, pltpu.HBM)


def call(kernel, outs, specs, scratch=(), limit=32 * 1024 * 1024):
    return pl.pallas_call(
        kernel,
        out_shape=outs,
        in_specs=specs,
        out_specs=jax.tree.map(lambda _: VMEM, outs),
        scratch_shapes=scratch,
        compiler_params=pltpu.CompilerParams(vmem_limit_bytes=limit),
    )


def head_rows(q_ref):
    q = jnp.concatenate([q_ref[r].astype(F32) for r in range(ROWS)], axis=0)
    return jnp.concatenate([q[:, h * HEAD : (h + 1) * HEAD] for h in range(GROUP)], axis=0)


def fetch(pairs, sems):
    copies = [pltpu.make_async_copy(s, d, sems.at[i]) for i, (s, d) in enumerate(pairs)]
    for copy in copies:
        copy.start()
    return copies


def tile_iota(dim):
    return lax.broadcasted_iota(jnp.int32, (TILE, HEAD), dim)


def upper():
    return tile_iota(0) >= STEPS


def by_request(side, apart):
    both = jnp.concatenate([side] * ROWS, axis=0)
    return jnp.where(upper(), pltpu.roll(both, HEAD - apart, axis=1), both)


def joined(message, h):
    at = h * ROWS * HEAD
    return jnp.concatenate(
        [message[:, at + r * HEAD : at + (r + 1) * HEAD] for r in range(ROWS)], axis=0
    )


def per_head(tile):
    return jnp.concatenate([tile] * GROUP, axis=0)


def soft_part(scores, valid):
    masked = [jnp.where(v, s, LOW) for s, v in zip(scores, valid)]
    tops = [jnp.max(s, axis=1, keepdims=True) for s in masked]
    top = functools.reduce(jnp.maximum, tops)
    weights = [jnp.where(v, jnp.exp(s - top), 0.0) for s, v in zip(masked, valid)]
    total = sum(jnp.sum(w, axis=1, keepdims=True) for w in weights)
    return top, total, weights


def dot_t(a, b):
    return lax.dot_general(a, b, (((1,), (1,)), ((), ())), preferred_element_type=F32)


def first_kernel(
    ctx_hbm,
    blocks_hbm,
    lender_hbm,
    q_hbm,
    nk_hbm,
    nv_hbm,
    k_hbm,
    v_hbm,
    lk_hbm,
    lv_hbm,
    out_ref,
    o_ref,
    m_ref,
    l_ref,
    pick_ref,
    lk_ref,
    lv_ref,
    ctx_ref,
    blocks_ref,
    lender_ref,
    q_ref,
    nk_ref,
    nv_ref,
    k_ref,
    v_ref,
    sems,
):
    pairs = [
        (q_hbm, q_ref),
        (k_hbm, k_ref),
        (lender_hbm, lender_ref),
        (ctx_hbm, ctx_ref),
        (blocks_hbm, blocks_ref),
        (nk_hbm, nk_ref),
        (v_hbm, v_ref),
        (nv_hbm, nv_ref),
        (lk_hbm, lk_ref),
        (lv_hbm, lv_ref),
    ]
    copies = fetch(pairs, sems)
    request, step, lane = tile_iota(0) // STEPS, tile_iota(0) % STEPS, tile_iota(1)

    copies[2].wait()
    lines = out_ref.shape[0]
    per_row = pick_ref.shape[0] // lines
    me = lax.axis_index("inst")
    row, col = me // per_row, me % per_row
    target = jnp.zeros((lines, HEAD), jnp.int32)
    for i, y in enumerate(LINE):
        here = lax.broadcasted_iota(jnp.int32, (lines, HEAD), 0) == i
        target = jnp.where(here, lender_ref[y * per_row + col] - row * per_row, target)
    for s, c in enumerate(ROW):
        pick_ref[s * lines : (s + 1) * lines] = jnp.where(target == c, 1.0, 0.0)

    for copy in [copies[0], *copies[3:5]]:
        copy.wait()
    q = head_rows(q_ref).astype(BF16)
    res_len, block_len = k_ref.shape[1], lk_ref.shape[1]
    side = jnp.zeros((STEPS, HEAD), F32)
    for r in range(ROWS):
        for i in range(blocks_ref.shape[1]):
            fill = jnp.clip(ctx_ref[r] - res_len - i * block_len, 0, block_len)
            hit = lane[:STEPS] == r * lk_ref.shape[0] + blocks_ref[r, i]
            side = jnp.where(hit, fill.astype(F32), side)
    steps = [q_ref[r].astype(F32) for r in range(ROWS)]
    tiles = [steps[r][:, h * HEAD : (h + 1) * HEAD] for h in range(GROUP) for r in range(ROWS)]
    message = jnp.concatenate([*tiles, side], axis=1).astype(BF16)
    for i in range(lines):
        out_ref[i] = message

    for copy in [copies[1], copies[5]]:
        copy.wait()
    scores, valid = [], []
    for r in range(ROWS):
        s = dot_t(q, k_ref[r]) * SCALE
        for c in range(res_len // HEAD):
            scores.append(s[:, c * HEAD : (c + 1) * HEAD])
            valid.append(per_head((request == r) & (lane + c * HEAD < ctx_ref[r])))
    blank = jnp.zeros((HEAD - TILE, HEAD), F32)

    def fresh(ref):
        return jnp.concatenate([ref[r].astype(F32) for r in range(ROWS)] + [blank], axis=0)

    scores.append(dot_t(q, fresh(nk_ref).astype(BF16)) * SCALE)
    valid.append(
        per_head((lane < TILE) & (lane // STEPS == request) & (lane % STEPS <= step))
    )
    top, total, weights = soft_part(scores, valid)
    for copy in copies[6:8]:
        copy.wait()
    w = [x.astype(BF16) for x in weights]
    acc = jnp.dot(w[-1], fresh(nv_ref).astype(BF16), preferred_element_type=F32)
    per = res_len // HEAD
    for r in range(ROWS):
        wide = jnp.concatenate(w[r * per : (r + 1) * per], axis=1)
        acc = acc + jnp.dot(wide, v_ref[r], preferred_element_type=F32)
    o_ref[...] = acc
    m_ref[...] = jnp.broadcast_to(top, m_ref.shape)
    l_ref[...] = jnp.broadcast_to(total, l_ref.shape)
    for copy in copies[8:]:
        copy.wait()


def place(pick_ref, in_ref, out_ref, place_of):
    held = []
    for i in range(in_ref.shape[0]):
        message = in_ref[i].astype(F32)
        side = jnp.concatenate([message[:, MSG - HEAD :]] * ROWS, axis=0)
        held.append([*(joined(message, h) for h in range(GROUP)), side])
    for o in range(out_ref.shape[0]):
        tiles = [jnp.zeros((TILE, HEAD), F32)] * (GROUP + 1)
        for i, message in enumerate(held):
            at = place_of(i, o)
            mine = jnp.broadcast_to(pick_ref[at : at + 1], (TILE, HEAD)) > 0.5
            tiles = [jnp.where(mine, m, tile) for m, tile in zip(message, tiles)]
        halves = [t[r * STEPS : (r + 1) * STEPS] for t in tiles[:GROUP] for r in range(ROWS)]
        out_ref[o] = jnp.concatenate([*halves, tiles[GROUP][:STEPS]], axis=1).astype(BF16)


def place_out_kernel(pick_ref, in_ref, out_ref):
    place(pick_ref, in_ref, out_ref, lambda y, s: s * in_ref.shape[0] + y)


def place_back_kernel(pick_ref, in_ref, out_ref):
    place(pick_ref, in_ref, out_ref, lambda s, y: s * out_ref.shape[0] + y)


def merged(in_ref):
    total = in_ref[0].astype(F32)
    for i in range(1, in_ref.shape[0]):
        total = total + in_ref[i].astype(F32)
    return total


def pieces(x, count):
    found = []
    for _ in range(count):
        piece = x.astype(BF16).astype(F32)
        found.append(piece)
        x = x - piece
    return found


def lent_kernel(in_ref, k_ref, v_ref, out_ref):
    message = merged(in_ref)
    q = jnp.concatenate([joined(message, h) for h in range(GROUP)], axis=0).astype(BF16)
    fills = by_request(message[:, MSG - HEAD :], k_ref.shape[0])
    block_len = k_ref.shape[1]
    k = k_ref[...].reshape(-1, HEAD)
    v = v_ref[...].reshape(-1, HEAD)
    s = dot_t(q, k) * SCALE
    lane = tile_iota(1).astype(F32)
    scores, valid = [], []
    for p in range(k_ref.shape[0]):
        scores.append(s[:, p * block_len : (p + 1) * block_len])
        valid.append(per_head(lane < fills[:, p : p + 1]))
    top, total, weights = soft_part(scores, valid)
    wide = jnp.concatenate([w.astype(BF16) for w in weights], axis=1)
    acc = jnp.dot(wide, v, preferred_element_type=F32)
    acc = acc * jnp.where(total > 0.0, 1.0 / jnp.maximum(total, 1e-30), 0.0)
    side = jnp.zeros((TILE, HEAD), F32)
    for h in range(GROUP):
        span = slice(h * TILE, (h + 1) * TILE)
        values = pieces(top[span], PARTS_M) + pieces(total[span], PARTS_L)
        for i, value in enumerate(values):
            side = jnp.where(tile_iota(1) == h * ROWS * PIECES + i, value, side)
    side = side[:STEPS] + pltpu.roll(side, PIECES, axis=1)[STEPS:]
    tiles = [acc[i * STEPS : (i + 1) * STEPS] for i in range(GROUP * ROWS)]
    reply = jnp.concatenate([*tiles, side], axis=1).astype(BF16)
    for i in range(out_ref.shape[0]):
        out_ref[i] = reply


def project_kernel(in_ref, o_ref, m_ref, l_ref, w_ref, out_ref):
    reply = merged(in_ref)
    side = by_request(reply[:, MSG - HEAD :], PIECES)
    heads = []
    for h in range(GROUP):
        span = slice(h * TILE, (h + 1) * TILE)
        first = h * ROWS * PIECES
        cols = [side[:, first + i : first + i + 1] for i in range(PIECES)]
        lent_top = cols[0] + cols[1] + cols[2]
        lent_total = cols[3] + cols[4]
        top = jnp.maximum(m_ref[span], lent_top)
        a = jnp.exp(m_ref[span] - top)
        b = jnp.exp(lent_top - top) * lent_total
        mixed = (a * o_ref[span] + b * joined(reply, h)) / (a * l_ref[span] + b)
        heads.append(mixed.astype(BF16))
    attended = jnp.concatenate(heads, axis=1)
    width = out_ref.shape[2]
    for i, x in enumerate(SHARD):
        out_ref[i] = jnp.dot(
            attended, w_ref[:, x * width : (x + 1) * width], preferred_element_type=F32
        )


def solution(mesh):
    insts, shards = mesh.shape["inst"], mesh.shape["tp"]
    per_row, lines = len(ROW), len(LINE)
    along_y = [[y * per_row + c for y in LINE] for c in range(per_row)]
    along_row = [[y * per_row + c for c in ROW] for y in range(lines)]

    def exchange(x, groups):
        return lax.all_to_all(x, "inst", 0, 0, axis_index_groups=groups, tiled=True)

    def local(
        queries,
        new_keys,
        new_values,
        res_keys,
        res_values,
        lendable_keys,
        lendable_values,
        ctx_len,
        blocks,
        lender,
        out_proj,
    ):
        def slots(n):
            return jax.ShapeDtypeStruct((n, STEPS, MSG), BF16)

        def like(x, space=pltpu.VMEM):
            return space(x.shape, x.dtype)

        def out_like(x):
            return jax.ShapeDtypeStruct(x.shape, x.dtype)

        numbers = (ctx_len, blocks, lender)
        given = (queries, new_keys, new_values, res_keys, res_values)
        lent = (lendable_keys, lendable_values)
        part = jax.ShapeDtypeStruct((QROWS, HEAD), F32)
        picks = jax.ShapeDtypeStruct((insts, HEAD), F32)
        outs = (slots(lines), part, part, part, picks, *map(out_like, lent))
        scratch = [
            *(like(x, pltpu.SMEM) for x in numbers),
            *map(like, given),
            pltpu.SemaphoreType.DMA((10,)),
        ]
        sent, *home, picked, lent_k, lent_v = call(first_kernel, outs, [HBM] * 10, scratch)(
            *map(off_chip, (*numbers, *given, *lent))
        )
        held = exchange(sent, along_y)
        placed = call(place_out_kernel, slots(per_row), [VMEM] * 2)(picked, held)
        arrived = exchange(placed, along_row)
        reply = call(lent_kernel, slots(per_row), [VMEM] * 3)(
            arrived, lent_k, lent_v
        )
        held_back = exchange(reply, along_row)
        placed_back = call(place_back_kernel, slots(lines), [VMEM] * 2)(picked, held_back)
        returned = exchange(placed_back, along_y)
        width = out_proj.shape[1] // shards
        terms = call(
            project_kernel,
            jax.ShapeDtypeStruct((shards, TILE, width), F32),
            [VMEM] * 5,
        )(returned, *home, out_proj)
        shares = lax.all_to_all(
            terms, "tp", 0, 0, axis_index_groups=[list(SHARD)], tiled=True
        )
        return jnp.sum(shares, axis=0).astype(BF16).reshape(ROWS, STEPS, width)

    in_specs = (
        P("inst", None, "tp"),
        P("inst", None, "tp"),
        P("inst", None, "tp"),
        P("inst", None, "tp"),
        P("inst", None, "tp"),
        P("inst", None, "tp"),
        P("inst", None, "tp"),
        P("inst"),
        P("inst", None),
        P(),
        P("tp", None),
    )
    out_specs = P("inst", None, "tp")
    return jax.shard_map(local, mesh=mesh, in_specs=in_specs, out_specs=out_specs, check_vma=False)
```

```python
import functools
import math

import jax
import jax.numpy as jnp
from jax import lax
from jax.experimental import pallas as pl
from jax.experimental.pallas import tpu as pltpu
from jax.sharding import PartitionSpec as P

HEAD = 128
GROUP = 5
ROWS = 2
STEPS = 4
TILE = ROWS * STEPS
QROWS = GROUP * TILE
PARTS = GROUP * ROWS + 1
MSG = PARTS * HEAD
LOW = -1e30
PARTS_M = 3
PARTS_L = 2
PIECES = PARTS_M + PARTS_L
SCALE = 1.0 / math.sqrt(HEAD)
LINE = (0, 4, 2, 6, 1, 5, 3, 7)
ROW = (0, 2, 4, 6, 9, 11, 13, 15, 1, 3, 5, 7, 8, 10, 12, 14)
SHARD = (0, 2, 1, 3)
F32 = jnp.float32
BF16 = jnp.bfloat16

VMEM = pl.BlockSpec(memory_space=pltpu.VMEM)
HBM = pl.BlockSpec(memory_space=pltpu.HBM)


def off_chip(x):
    return pltpu.with_memory_space_constraint(x, pltpu.HBM)


def call(kernel, outs, specs, scratch=(), limit=32 * 1024 * 1024):
    return pl.pallas_call(
        kernel,
        out_shape=outs,
        in_specs=specs,
        out_specs=jax.tree.map(lambda _: VMEM, outs),
        scratch_shapes=scratch,
        compiler_params=pltpu.CompilerParams(vmem_limit_bytes=limit),
    )


def head_rows(q_ref):
    q = jnp.concatenate([q_ref[r].astype(F32) for r in range(ROWS)], axis=0)
    return jnp.concatenate([q[:, h * HEAD : (h + 1) * HEAD] for h in range(GROUP)], axis=0)


def fetch(pairs, sems):
    copies = [pltpu.make_async_copy(s, d, sems.at[i]) for i, (s, d) in enumerate(pairs)]
    for copy in copies:
        copy.start()
    return copies


def tile_iota(dim):
    return lax.broadcasted_iota(jnp.int32, (TILE, HEAD), dim)


def upper():
    return tile_iota(0) >= STEPS


def by_request(side, apart):
    both = jnp.concatenate([side] * ROWS, axis=0)
    return jnp.where(upper(), pltpu.roll(both, HEAD - apart, axis=1), both)


def joined(message, h):
    at = h * ROWS * HEAD
    return jnp.concatenate(
        [message[:, at + r * HEAD : at + (r + 1) * HEAD] for r in range(ROWS)], axis=0
    )


def per_head(tile):
    return jnp.concatenate([tile] * GROUP, axis=0)


def soft_part(scores, valid):
    masked = [jnp.where(v, s, LOW) for s, v in zip(scores, valid)]
    tops = [jnp.max(s, axis=1, keepdims=True) for s in masked]
    top = functools.reduce(jnp.maximum, tops)
    weights = [jnp.where(v, jnp.exp(s - top), 0.0) for s, v in zip(masked, valid)]
    total = sum(jnp.sum(w, axis=1, keepdims=True) for w in weights)
    return top, total, weights


def dot_t(a, b):
    return lax.dot_general(a, b, (((1,), (1,)), ((), ())), preferred_element_type=F32)


def first_kernel(
    ctx_hbm,
    blocks_hbm,
    lender_hbm,
    q_hbm,
    nk_hbm,
    nv_hbm,
    k_hbm,
    v_hbm,
    lk_hbm,
    lv_hbm,
    out_ref,
    o_ref,
    m_ref,
    l_ref,
    pick_ref,
    lk_ref,
    lv_ref,
    ctx_ref,
    blocks_ref,
    lender_ref,
    q_ref,
    nk_ref,
    nv_ref,
    k_ref,
    v_ref,
    sems,
):
    pairs = [
        (q_hbm, q_ref),
        (k_hbm, k_ref),
        (lender_hbm, lender_ref),
        (ctx_hbm, ctx_ref),
        (blocks_hbm, blocks_ref),
        (nk_hbm, nk_ref),
        (v_hbm, v_ref),
        (nv_hbm, nv_ref),
        (lk_hbm, lk_ref),
        (lv_hbm, lv_ref),
    ]
    copies = fetch(pairs, sems)
    request, step, lane = tile_iota(0) // STEPS, tile_iota(0) % STEPS, tile_iota(1)

    copies[2].wait()
    lines = out_ref.shape[0]
    per_row = pick_ref.shape[0] // lines
    me = lax.axis_index("inst")
    row, col = me // per_row, me % per_row
    target = jnp.zeros((lines, HEAD), jnp.int32)
    for i, y in enumerate(LINE):
        here = lax.broadcasted_iota(jnp.int32, (lines, HEAD), 0) == i
        target = jnp.where(here, lender_ref[y * per_row + col] - row * per_row, target)
    for s, c in enumerate(ROW):
        pick_ref[s * lines : (s + 1) * lines] = jnp.where(target == c, 1.0, 0.0)

    for copy in [copies[0], *copies[3:5]]:
        copy.wait()
    q = head_rows(q_ref).astype(BF16)
    res_len, block_len = k_ref.shape[1], lk_ref.shape[1]
    side = jnp.zeros((STEPS, HEAD), F32)
    for r in range(ROWS):
        for i in range(blocks_ref.shape[1]):
            fill = jnp.clip(ctx_ref[r] - res_len - i * block_len, 0, block_len)
            hit = lane[:STEPS] == r * lk_ref.shape[0] + blocks_ref[r, i]
            side = jnp.where(hit, fill.astype(F32), side)
    steps = [q_ref[r].astype(F32) for r in range(ROWS)]
    tiles = [steps[r][:, h * HEAD : (h + 1) * HEAD] for h in range(GROUP) for r in range(ROWS)]
    message = jnp.concatenate([*tiles, side], axis=1).astype(BF16)
    for i in range(lines):
        out_ref[i] = message

    for copy in [copies[1], copies[5]]:
        copy.wait()
    scores, valid = [], []
    for r in range(ROWS):
        s = dot_t(q, k_ref[r]) * SCALE
        for c in range(res_len // HEAD):
            scores.append(s[:, c * HEAD : (c + 1) * HEAD])
            valid.append(per_head((request == r) & (lane + c * HEAD < ctx_ref[r])))
    blank = jnp.zeros((HEAD - TILE, HEAD), F32)

    def fresh(ref):
        return jnp.concatenate([ref[r].astype(F32) for r in range(ROWS)] + [blank], axis=0)

    scores.append(dot_t(q, fresh(nk_ref).astype(BF16)) * SCALE)
    valid.append(
        per_head((lane < TILE) & (lane // STEPS == request) & (lane % STEPS <= step))
    )
    top, total, weights = soft_part(scores, valid)
    for copy in copies[6:8]:
        copy.wait()
    w = [x.astype(BF16) for x in weights]
    acc = jnp.dot(w[-1], fresh(nv_ref).astype(BF16), preferred_element_type=F32)
    per = res_len // HEAD
    for r in range(ROWS):
        wide = jnp.concatenate(w[r * per : (r + 1) * per], axis=1)
        acc = acc + jnp.dot(wide, v_ref[r], preferred_element_type=F32)
    o_ref[...] = acc
    m_ref[...] = jnp.broadcast_to(top, m_ref.shape)
    l_ref[...] = jnp.broadcast_to(total, l_ref.shape)
    for copy in copies[8:]:
        copy.wait()


def place(pick_ref, in_ref, out_ref, place_of):
    held = []
    for i in range(in_ref.shape[0]):
        message = in_ref[i].astype(F32)
        side = jnp.concatenate([message[:, MSG - HEAD :]] * ROWS, axis=0)
        held.append([*(joined(message, h) for h in range(GROUP)), side])
    for o in range(out_ref.shape[0]):
        tiles = [jnp.zeros((TILE, HEAD), F32)] * (GROUP + 1)
        for i, message in enumerate(held):
            at = place_of(i, o)
            mine = jnp.broadcast_to(pick_ref[at : at + 1], (TILE, HEAD)) > 0.5
            tiles = [jnp.where(mine, m, tile) for m, tile in zip(message, tiles)]
        halves = [t[r * STEPS : (r + 1) * STEPS] for t in tiles[:GROUP] for r in range(ROWS)]
        out_ref[o] = jnp.concatenate([*halves, tiles[GROUP][:STEPS]], axis=1).astype(BF16)


def place_out_kernel(pick_ref, in_ref, out_ref):
    place(pick_ref, in_ref, out_ref, lambda y, s: s * in_ref.shape[0] + y)


def place_back_kernel(pick_ref, in_ref, out_ref):
    place(pick_ref, in_ref, out_ref, lambda s, y: s * out_ref.shape[0] + y)


def merged(in_ref):
    total = in_ref[0].astype(F32)
    for i in range(1, in_ref.shape[0]):
        total = total + in_ref[i].astype(F32)
    return total


def pieces(x, count):
    found = []
    for _ in range(count):
        piece = x.astype(BF16).astype(F32)
        found.append(piece)
        x = x - piece
    return found


def lent_kernel(in_ref, k_ref, v_ref, out_ref):
    message = merged(in_ref)
    q = jnp.concatenate([joined(message, h) for h in range(GROUP)], axis=0).astype(BF16)
    fills = by_request(message[:, MSG - HEAD :], k_ref.shape[0])
    block_len = k_ref.shape[1]
    k = k_ref[...].reshape(-1, HEAD)
    v = v_ref[...].reshape(-1, HEAD)
    s = dot_t(q, k) * SCALE
    lane = tile_iota(1).astype(F32)
    scores, valid = [], []
    for p in range(k_ref.shape[0]):
        scores.append(s[:, p * block_len : (p + 1) * block_len])
        valid.append(per_head(lane < fills[:, p : p + 1]))
    top, total, weights = soft_part(scores, valid)
    wide = jnp.concatenate([w.astype(BF16) for w in weights], axis=1)
    acc = jnp.dot(wide, v, preferred_element_type=F32)
    acc = acc * jnp.where(total > 0.0, 1.0 / jnp.maximum(total, 1e-30), 0.0)
    side = jnp.zeros((TILE, HEAD), F32)
    for h in range(GROUP):
        span = slice(h * TILE, (h + 1) * TILE)
        values = pieces(top[span], PARTS_M) + pieces(total[span], PARTS_L)
        for i, value in enumerate(values):
            side = jnp.where(tile_iota(1) == h * ROWS * PIECES + i, value, side)
    side = side[:STEPS] + pltpu.roll(side, PIECES, axis=1)[STEPS:]
    tiles = [acc[i * STEPS : (i + 1) * STEPS] for i in range(GROUP * ROWS)]
    reply = jnp.concatenate([*tiles, side], axis=1).astype(BF16)
    for i in range(out_ref.shape[0]):
        out_ref[i] = reply


def project_kernel(in_ref, o_ref, m_ref, l_ref, w_ref, out_ref):
    reply = merged(in_ref)
    side = by_request(reply[:, MSG - HEAD :], PIECES)
    heads = []
    for h in range(GROUP):
        span = slice(h * TILE, (h + 1) * TILE)
        first = h * ROWS * PIECES
        cols = [side[:, first + i : first + i + 1] for i in range(PIECES)]
        lent_top = cols[0] + cols[1] + cols[2]
        lent_total = cols[3] + cols[4]
        top = jnp.maximum(m_ref[span], lent_top)
        a = jnp.exp(m_ref[span] - top)
        b = jnp.exp(lent_top - top) * lent_total
        mixed = (a * o_ref[span] + b * joined(reply, h)) / (a * l_ref[span] + b)
        heads.append(mixed.astype(BF16))
    attended = jnp.concatenate(heads, axis=1)
    width = out_ref.shape[2]
    for i, x in enumerate(SHARD):
        out_ref[i] = jnp.dot(
            attended, w_ref[:, x * width : (x + 1) * width], preferred_element_type=F32
        )


def solution(mesh):
    insts, shards = mesh.shape["inst"], mesh.shape["tp"]
    per_row, lines = len(ROW), len(LINE)
    along_y = [[y * per_row + c for y in LINE] for c in range(per_row)]
    along_row = [[y * per_row + c for c in ROW] for y in range(lines)]

    def exchange(x, groups):
        return lax.all_to_all(x, "inst", 0, 0, axis_index_groups=groups, tiled=True)

    def local(
        queries,
        new_keys,
        new_values,
        res_keys,
        res_values,
        lendable_keys,
        lendable_values,
        ctx_len,
        blocks,
        lender,
        out_proj,
    ):
        def slots(n):
            return jax.ShapeDtypeStruct((n, STEPS, MSG), BF16)

        def like(x, space=pltpu.VMEM):
            return space(x.shape, x.dtype)

        def out_like(x):
            return jax.ShapeDtypeStruct(x.shape, x.dtype)

        numbers = (ctx_len, blocks, lender)
        given = (queries, new_keys, new_values, res_keys, res_values)
        lent = (lendable_keys, lendable_values)
        part = jax.ShapeDtypeStruct((QROWS, HEAD), F32)
        picks = jax.ShapeDtypeStruct((insts, HEAD), F32)
        outs = (slots(lines), part, part, part, picks, *map(out_like, lent))
        scratch = [
            *(like(x, pltpu.SMEM) for x in numbers),
            *map(like, given),
            pltpu.SemaphoreType.DMA((10,)),
        ]
        sent, *home, picked, lent_k, lent_v = call(first_kernel, outs, [HBM] * 10, scratch)(
            *map(off_chip, (*numbers, *given, *lent))
        )
        held = exchange(sent, along_y)
        placed = call(place_out_kernel, slots(per_row), [VMEM] * 2)(picked, held)
        arrived = exchange(placed, along_row)
        reply = call(lent_kernel, slots(per_row), [VMEM] * 3)(
            arrived, lent_k, lent_v
        )
        held_back = exchange(reply, along_row)
        placed_back = call(place_back_kernel, slots(lines), [VMEM] * 2)(picked, held_back)
        returned = exchange(placed_back, along_y)
        width = out_proj.shape[1] // shards
        terms = call(
            project_kernel,
            jax.ShapeDtypeStruct((shards, TILE, width), F32),
            [VMEM] * 5,
        )(returned, *home, out_proj)
        shares = lax.all_to_all(
            terms, "tp", 0, 0, axis_index_groups=[list(SHARD)], tiled=True
        )
        return jnp.sum(shares, axis=0).astype(BF16).reshape(ROWS, STEPS, width)

    in_specs = (
        P("inst", None, "tp"),
        P("inst", None, "tp"),
        P("inst", None, "tp"),
        P("inst", None, "tp"),
        P("inst", None, "tp"),
        P("inst", None, "tp"),
        P("inst", None, "tp"),
        P("inst"),
        P("inst", None),
        P(),
        P("tp", None),
    )
    out_specs = P("inst", None, "tp")
    return jax.shard_map(local, mesh=mesh, in_specs=in_specs, out_specs=out_specs, check_vma=False)
```

```python
import functools
import math

import jax
import jax.numpy as jnp
from jax import lax
from jax.experimental import pallas as pl
from jax.experimental.pallas import tpu as pltpu
from jax.sharding import PartitionSpec as P

HEAD = 128
GROUP = 5
ROWS = 2
STEPS = 4
TILE = ROWS * STEPS
QROWS = GROUP * TILE
PARTS = GROUP * ROWS + 1
MSG = PARTS * HEAD
LOW = -1e30
PARTS_M = 3
PARTS_L = 2
PIECES = PARTS_M + PARTS_L
SCALE = 1.0 / math.sqrt(HEAD)
LINE = (0, 4, 2, 6, 1, 5, 3, 7)
ROW = (0, 2, 9, 11, 4, 6, 13, 15, 1, 3, 8, 10, 5, 7, 12, 14)
SHARD = (0, 1, 3, 2)
F32 = jnp.float32
BF16 = jnp.bfloat16

VMEM = pl.BlockSpec(memory_space=pltpu.VMEM)
HBM = pl.BlockSpec(memory_space=pltpu.HBM)


def off_chip(x):
    return pltpu.with_memory_space_constraint(x, pltpu.HBM)


def call(kernel, outs, specs, scratch=(), limit=32 * 1024 * 1024):
    return pl.pallas_call(
        kernel,
        out_shape=outs,
        in_specs=specs,
        out_specs=jax.tree.map(lambda _: VMEM, outs),
        scratch_shapes=scratch,
        compiler_params=pltpu.CompilerParams(vmem_limit_bytes=limit),
    )


def head_rows(q_ref):
    q = jnp.concatenate([q_ref[r].astype(F32) for r in range(ROWS)], axis=0)
    return jnp.concatenate([q[:, h * HEAD : (h + 1) * HEAD] for h in range(GROUP)], axis=0)


def fetch(pairs, sems):
    copies = [pltpu.make_async_copy(s, d, sems.at[i]) for i, (s, d) in enumerate(pairs)]
    for copy in copies:
        copy.start()
    return copies


def tile_iota(dim):
    return lax.broadcasted_iota(jnp.int32, (TILE, HEAD), dim)


def upper():
    return tile_iota(0) >= STEPS


def by_request(side, apart):
    both = jnp.concatenate([side] * ROWS, axis=0)
    return jnp.where(upper(), pltpu.roll(both, HEAD - apart, axis=1), both)


def joined(message, h):
    at = h * ROWS * HEAD
    return jnp.concatenate(
        [message[:, at + r * HEAD : at + (r + 1) * HEAD] for r in range(ROWS)], axis=0
    )


def per_head(tile):
    return jnp.concatenate([tile] * GROUP, axis=0)


def soft_part(scores, valid):
    masked = [jnp.where(v, s, LOW) for s, v in zip(scores, valid)]
    tops = [jnp.max(s, axis=1, keepdims=True) for s in masked]
    top = functools.reduce(jnp.maximum, tops)
    weights = [jnp.where(v, jnp.exp(s - top), 0.0) for s, v in zip(masked, valid)]
    total = sum(jnp.sum(w, axis=1, keepdims=True) for w in weights)
    return top, total, weights


def dot_t(a, b):
    return lax.dot_general(a, b, (((1,), (1,)), ((), ())), preferred_element_type=F32)


def first_kernel(
    ctx_hbm,
    blocks_hbm,
    lender_hbm,
    q_hbm,
    nk_hbm,
    nv_hbm,
    k_hbm,
    v_hbm,
    lk_hbm,
    lv_hbm,
    out_ref,
    o_ref,
    m_ref,
    l_ref,
    pick_ref,
    lk_ref,
    lv_ref,
    ctx_ref,
    blocks_ref,
    lender_ref,
    q_ref,
    nk_ref,
    nv_ref,
    k_ref,
    v_ref,
    sems,
):
    pairs = [
        (q_hbm, q_ref),
        (k_hbm, k_ref),
        (lender_hbm, lender_ref),
        (ctx_hbm, ctx_ref),
        (blocks_hbm, blocks_ref),
        (nk_hbm, nk_ref),
        (v_hbm, v_ref),
        (nv_hbm, nv_ref),
        (lk_hbm, lk_ref),
        (lv_hbm, lv_ref),
    ]
    copies = fetch(pairs, sems)
    request, step, lane = tile_iota(0) // STEPS, tile_iota(0) % STEPS, tile_iota(1)

    copies[2].wait()
    lines = out_ref.shape[0]
    per_row = pick_ref.shape[0] // lines
    me = lax.axis_index("inst")
    row, col = me // per_row, me % per_row
    target = jnp.zeros((lines, HEAD), jnp.int32)
    for i, y in enumerate(LINE):
        here = lax.broadcasted_iota(jnp.int32, (lines, HEAD), 0) == i
        target = jnp.where(here, lender_ref[y * per_row + col] - row * per_row, target)
    for s, c in enumerate(ROW):
        pick_ref[s * lines : (s + 1) * lines] = jnp.where(target == c, 1.0, 0.0)

    for copy in [copies[0], *copies[3:5]]:
        copy.wait()
    q = head_rows(q_ref).astype(BF16)
    res_len, block_len = k_ref.shape[1], lk_ref.shape[1]
    side = jnp.zeros((STEPS, HEAD), F32)
    for r in range(ROWS):
        for i in range(blocks_ref.shape[1]):
            fill = jnp.clip(ctx_ref[r] - res_len - i * block_len, 0, block_len)
            hit = lane[:STEPS] == r * lk_ref.shape[0] + blocks_ref[r, i]
            side = jnp.where(hit, fill.astype(F32), side)
    steps = [q_ref[r].astype(F32) for r in range(ROWS)]
    tiles = [steps[r][:, h * HEAD : (h + 1) * HEAD] for h in range(GROUP) for r in range(ROWS)]
    message = jnp.concatenate([*tiles, side], axis=1).astype(BF16)
    for i in range(lines):
        out_ref[i] = message

    for copy in [copies[1], copies[5]]:
        copy.wait()
    scores, valid = [], []
    for r in range(ROWS):
        s = dot_t(q, k_ref[r]) * SCALE
        for c in range(res_len // HEAD):
            scores.append(s[:, c * HEAD : (c + 1) * HEAD])
            valid.append(per_head((request == r) & (lane + c * HEAD < ctx_ref[r])))
    blank = jnp.zeros((HEAD - TILE, HEAD), F32)

    def fresh(ref):
        return jnp.concatenate([ref[r].astype(F32) for r in range(ROWS)] + [blank], axis=0)

    scores.append(dot_t(q, fresh(nk_ref).astype(BF16)) * SCALE)
    valid.append(
        per_head((lane < TILE) & (lane // STEPS == request) & (lane % STEPS <= step))
    )
    top, total, weights = soft_part(scores, valid)
    for copy in copies[6:8]:
        copy.wait()
    w = [x.astype(BF16) for x in weights]
    acc = jnp.dot(w[-1], fresh(nv_ref).astype(BF16), preferred_element_type=F32)
    per = res_len // HEAD
    for r in range(ROWS):
        wide = jnp.concatenate(w[r * per : (r + 1) * per], axis=1)
        acc = acc + jnp.dot(wide, v_ref[r], preferred_element_type=F32)
    o_ref[...] = acc
    m_ref[...] = jnp.broadcast_to(top, m_ref.shape)
    l_ref[...] = jnp.broadcast_to(total, l_ref.shape)
    for copy in copies[8:]:
        copy.wait()


def place(pick_ref, in_ref, out_ref, place_of):
    held = []
    for i in range(in_ref.shape[0]):
        message = in_ref[i].astype(F32)
        side = jnp.concatenate([message[:, MSG - HEAD :]] * ROWS, axis=0)
        held.append([*(joined(message, h) for h in range(GROUP)), side])
    for o in range(out_ref.shape[0]):
        tiles = [jnp.zeros((TILE, HEAD), F32)] * (GROUP + 1)
        for i, message in enumerate(held):
            at = place_of(i, o)
            mine = jnp.broadcast_to(pick_ref[at : at + 1], (TILE, HEAD)) > 0.5
            tiles = [jnp.where(mine, m, tile) for m, tile in zip(message, tiles)]
        halves = [t[r * STEPS : (r + 1) * STEPS] for t in tiles[:GROUP] for r in range(ROWS)]
        out_ref[o] = jnp.concatenate([*halves, tiles[GROUP][:STEPS]], axis=1).astype(BF16)


def place_out_kernel(pick_ref, in_ref, out_ref):
    place(pick_ref, in_ref, out_ref, lambda y, s: s * in_ref.shape[0] + y)


def place_back_kernel(pick_ref, in_ref, out_ref):
    place(pick_ref, in_ref, out_ref, lambda s, y: s * out_ref.shape[0] + y)


def merged(in_ref):
    total = in_ref[0].astype(F32)
    for i in range(1, in_ref.shape[0]):
        total = total + in_ref[i].astype(F32)
    return total


def pieces(x, count):
    found = []
    for _ in range(count):
        piece = x.astype(BF16).astype(F32)
        found.append(piece)
        x = x - piece
    return found


def lent_kernel(in_ref, k_ref, v_ref, out_ref):
    message = merged(in_ref)
    q = jnp.concatenate([joined(message, h) for h in range(GROUP)], axis=0).astype(BF16)
    fills = by_request(message[:, MSG - HEAD :], k_ref.shape[0])
    block_len = k_ref.shape[1]
    k = k_ref[...].reshape(-1, HEAD)
    v = v_ref[...].reshape(-1, HEAD)
    s = dot_t(q, k) * SCALE
    lane = tile_iota(1).astype(F32)
    scores, valid = [], []
    for p in range(k_ref.shape[0]):
        scores.append(s[:, p * block_len : (p + 1) * block_len])
        valid.append(per_head(lane < fills[:, p : p + 1]))
    top, total, weights = soft_part(scores, valid)
    wide = jnp.concatenate([w.astype(BF16) for w in weights], axis=1)
    acc = jnp.dot(wide, v, preferred_element_type=F32)
    acc = acc * jnp.where(total > 0.0, 1.0 / jnp.maximum(total, 1e-30), 0.0)
    side = jnp.zeros((TILE, HEAD), F32)
    for h in range(GROUP):
        span = slice(h * TILE, (h + 1) * TILE)
        values = pieces(top[span], PARTS_M) + pieces(total[span], PARTS_L)
        for i, value in enumerate(values):
            side = jnp.where(tile_iota(1) == h * ROWS * PIECES + i, value, side)
    side = side[:STEPS] + pltpu.roll(side, PIECES, axis=1)[STEPS:]
    tiles = [acc[i * STEPS : (i + 1) * STEPS] for i in range(GROUP * ROWS)]
    reply = jnp.concatenate([*tiles, side], axis=1).astype(BF16)
    for i in range(out_ref.shape[0]):
        out_ref[i] = reply


def project_kernel(in_ref, o_ref, m_ref, l_ref, w_ref, out_ref):
    reply = merged(in_ref)
    side = by_request(reply[:, MSG - HEAD :], PIECES)
    heads = []
    for h in range(GROUP):
        span = slice(h * TILE, (h + 1) * TILE)
        first = h * ROWS * PIECES
        cols = [side[:, first + i : first + i + 1] for i in range(PIECES)]
        lent_top = cols[0] + cols[1] + cols[2]
        lent_total = cols[3] + cols[4]
        top = jnp.maximum(m_ref[span], lent_top)
        a = jnp.exp(m_ref[span] - top)
        b = jnp.exp(lent_top - top) * lent_total
        mixed = (a * o_ref[span] + b * joined(reply, h)) / (a * l_ref[span] + b)
        heads.append(mixed.astype(BF16))
    attended = jnp.concatenate(heads, axis=1)
    width = out_ref.shape[2]
    for i, x in enumerate(SHARD):
        out_ref[i] = jnp.dot(
            attended, w_ref[:, x * width : (x + 1) * width], preferred_element_type=F32
        )


def solution(mesh):
    insts, shards = mesh.shape["inst"], mesh.shape["tp"]
    per_row, lines = len(ROW), len(LINE)
    along_y = [[y * per_row + c for y in LINE] for c in range(per_row)]
    along_row = [[y * per_row + c for c in ROW] for y in range(lines)]

    def exchange(x, groups):
        return lax.all_to_all(x, "inst", 0, 0, axis_index_groups=groups, tiled=True)

    def local(
        queries,
        new_keys,
        new_values,
        res_keys,
        res_values,
        lendable_keys,
        lendable_values,
        ctx_len,
        blocks,
        lender,
        out_proj,
    ):
        def slots(n):
            return jax.ShapeDtypeStruct((n, STEPS, MSG), BF16)

        def like(x, space=pltpu.VMEM):
            return space(x.shape, x.dtype)

        def out_like(x):
            return jax.ShapeDtypeStruct(x.shape, x.dtype)

        numbers = (ctx_len, blocks, lender)
        given = (queries, new_keys, new_values, res_keys, res_values)
        lent = (lendable_keys, lendable_values)
        part = jax.ShapeDtypeStruct((QROWS, HEAD), F32)
        picks = jax.ShapeDtypeStruct((insts, HEAD), F32)
        outs = (slots(lines), part, part, part, picks, *map(out_like, lent))
        scratch = [
            *(like(x, pltpu.SMEM) for x in numbers),
            *map(like, given),
            pltpu.SemaphoreType.DMA((10,)),
        ]
        sent, *home, picked, lent_k, lent_v = call(first_kernel, outs, [HBM] * 10, scratch)(
            *map(off_chip, (*numbers, *given, *lent))
        )
        held = exchange(sent, along_y)
        placed = call(place_out_kernel, slots(per_row), [VMEM] * 2)(picked, held)
        arrived = exchange(placed, along_row)
        reply = call(lent_kernel, slots(per_row), [VMEM] * 3)(
            arrived, lent_k, lent_v
        )
        held_back = exchange(reply, along_row)
        placed_back = call(place_back_kernel, slots(lines), [VMEM] * 2)(picked, held_back)
        returned = exchange(placed_back, along_y)
        width = out_proj.shape[1] // shards
        terms = call(
            project_kernel,
            jax.ShapeDtypeStruct((shards, TILE, width), F32),
            [VMEM] * 5,
        )(returned, *home, out_proj)
        shares = lax.all_to_all(
            terms, "tp", 0, 0, axis_index_groups=[list(SHARD)], tiled=True
        )
        return jnp.sum(shares, axis=0).astype(BF16).reshape(ROWS, STEPS, width)

    in_specs = (
        P("inst", None, "tp"),
        P("inst", None, "tp"),
        P("inst", None, "tp"),
        P("inst", None, "tp"),
        P("inst", None, "tp"),
        P("inst", None, "tp"),
        P("inst", None, "tp"),
        P("inst"),
        P("inst", None),
        P(),
        P("tp", None),
    )
    out_specs = P("inst", None, "tp")
    return jax.shard_map(local, mesh=mesh, in_specs=in_specs, out_specs=out_specs, check_vma=False)
```

```python
import functools
import math

import jax
import jax.numpy as jnp
from jax import lax
from jax.experimental import pallas as pl
from jax.experimental.pallas import tpu as pltpu
from jax.sharding import PartitionSpec as P

HEAD = 128
GROUP = 5
ROWS = 2
STEPS = 4
TILE = ROWS * STEPS
QROWS = GROUP * TILE
PARTS = GROUP * ROWS + 1
MSG = PARTS * HEAD
LOW = -1e30
PARTS_M = 3
PARTS_L = 2
PIECES = PARTS_M + PARTS_L
SCALE = 1.0 / math.sqrt(HEAD)
LINE = (0, 4, 2, 6, 1, 5, 3, 7)
ROW = (0, 2, 9, 11, 4, 6, 13, 15, 1, 3, 8, 10, 5, 7, 12, 14)
SHARD = (0, 1, 3, 2)
F32 = jnp.float32
BF16 = jnp.bfloat16

VMEM = pl.BlockSpec(memory_space=pltpu.VMEM)
HBM = pl.BlockSpec(memory_space=pltpu.HBM)


def off_chip(x):
    return pltpu.with_memory_space_constraint(x, pltpu.HBM)


def call(kernel, outs, specs, scratch=(), limit=32 * 1024 * 1024):
    return pl.pallas_call(
        kernel,
        out_shape=outs,
        in_specs=specs,
        out_specs=jax.tree.map(lambda _: VMEM, outs),
        scratch_shapes=scratch,
        compiler_params=pltpu.CompilerParams(vmem_limit_bytes=limit),
    )


def head_rows(q_ref):
    q = jnp.concatenate([q_ref[r].astype(F32) for r in range(ROWS)], axis=0)
    return jnp.concatenate([q[:, h * HEAD : (h + 1) * HEAD] for h in range(GROUP)], axis=0)


def fetch(pairs, sems):
    copies = [pltpu.make_async_copy(s, d, sems.at[i]) for i, (s, d) in enumerate(pairs)]
    for copy in copies:
        copy.start()
    return copies


def tile_iota(dim):
    return lax.broadcasted_iota(jnp.int32, (TILE, HEAD), dim)


def upper():
    return tile_iota(0) >= STEPS


def by_request(side, apart):
    both = jnp.concatenate([side] * ROWS, axis=0)
    return jnp.where(upper(), pltpu.roll(both, HEAD - apart, axis=1), both)


def joined(message, h):
    at = h * ROWS * HEAD
    return jnp.concatenate(
        [message[:, at + r * HEAD : at + (r + 1) * HEAD] for r in range(ROWS)], axis=0
    )


def per_head(tile):
    return jnp.concatenate([tile] * GROUP, axis=0)


def soft_part(scores, valid):
    masked = [jnp.where(v, s, LOW) for s, v in zip(scores, valid)]
    tops = [jnp.max(s, axis=1, keepdims=True) for s in masked]
    top = functools.reduce(jnp.maximum, tops)
    weights = [jnp.where(v, jnp.exp(s - top), 0.0) for s, v in zip(masked, valid)]
    total = sum(jnp.sum(w, axis=1, keepdims=True) for w in weights)
    return top, total, weights


def dot_t(a, b):
    return lax.dot_general(a, b, (((1,), (1,)), ((), ())), preferred_element_type=F32)


def first_kernel(
    ctx_hbm,
    blocks_hbm,
    lender_hbm,
    q_hbm,
    nk_hbm,
    nv_hbm,
    k_hbm,
    v_hbm,
    lk_hbm,
    lv_hbm,
    out_ref,
    o_ref,
    m_ref,
    l_ref,
    pick_ref,
    lk_ref,
    lv_ref,
    ctx_ref,
    blocks_ref,
    lender_ref,
    q_ref,
    nk_ref,
    nv_ref,
    k_ref,
    v_ref,
    sems,
):
    pairs = [
        (q_hbm, q_ref),
        (k_hbm, k_ref),
        (lender_hbm, lender_ref),
        (ctx_hbm, ctx_ref),
        (blocks_hbm, blocks_ref),
        (nk_hbm, nk_ref),
        (v_hbm, v_ref),
        (nv_hbm, nv_ref),
        (lk_hbm, lk_ref),
        (lv_hbm, lv_ref),
    ]
    copies = fetch(pairs, sems)
    request, step, lane = tile_iota(0) // STEPS, tile_iota(0) % STEPS, tile_iota(1)

    copies[2].wait()
    lines = out_ref.shape[0]
    per_row = pick_ref.shape[0] // lines
    me = lax.axis_index("inst")
    row, col = me // per_row, me % per_row
    target = jnp.zeros((lines, HEAD), jnp.int32)
    for i, y in enumerate(LINE):
        here = lax.broadcasted_iota(jnp.int32, (lines, HEAD), 0) == i
        target = jnp.where(here, lender_ref[y * per_row + col] - row * per_row, target)
    for s, c in enumerate(ROW):
        pick_ref[s * lines : (s + 1) * lines] = jnp.where(target == c, 1.0, 0.0)

    for copy in [copies[0], *copies[3:5]]:
        copy.wait()
    q = head_rows(q_ref).astype(BF16)
    res_len, block_len = k_ref.shape[1], lk_ref.shape[1]
    side = jnp.zeros((STEPS, HEAD), F32)
    for r in range(ROWS):
        for i in range(blocks_ref.shape[1]):
            fill = jnp.clip(ctx_ref[r] - res_len - i * block_len, 0, block_len)
            hit = lane[:STEPS] == r * lk_ref.shape[0] + blocks_ref[r, i]
            side = jnp.where(hit, fill.astype(F32), side)
    steps = [q_ref[r].astype(F32) for r in range(ROWS)]
    tiles = [steps[r][:, h * HEAD : (h + 1) * HEAD] for h in range(GROUP) for r in range(ROWS)]
    message = jnp.concatenate([*tiles, side], axis=1).astype(BF16)
    for i in range(lines):
        out_ref[i] = message

    for copy in [copies[1], copies[5]]:
        copy.wait()
    scores, valid = [], []
    for r in range(ROWS):
        s = dot_t(q, k_ref[r]) * SCALE
        for c in range(res_len // HEAD):
            scores.append(s[:, c * HEAD : (c + 1) * HEAD])
            valid.append(per_head((request == r) & (lane + c * HEAD < ctx_ref[r])))
    blank = jnp.zeros((HEAD - TILE, HEAD), F32)

    def fresh(ref):
        return jnp.concatenate([ref[r].astype(F32) for r in range(ROWS)] + [blank], axis=0)

    scores.append(dot_t(q, fresh(nk_ref).astype(BF16)) * SCALE)
    valid.append(
        per_head((lane < TILE) & (lane // STEPS == request) & (lane % STEPS <= step))
    )
    top, total, weights = soft_part(scores, valid)
    for copy in copies[6:8]:
        copy.wait()
    w = [x.astype(BF16) for x in weights]
    acc = jnp.dot(w[-1], fresh(nv_ref).astype(BF16), preferred_element_type=F32)
    per = res_len // HEAD
    for r in range(ROWS):
        wide = jnp.concatenate(w[r * per : (r + 1) * per], axis=1)
        acc = acc + jnp.dot(wide, v_ref[r], preferred_element_type=F32)
    o_ref[...] = acc
    m_ref[...] = jnp.broadcast_to(top, m_ref.shape)
    l_ref[...] = jnp.broadcast_to(total, l_ref.shape)
    for copy in copies[8:]:
        copy.wait()


def place(pick_ref, in_ref, out_ref, place_of):
    held = []
    for i in range(in_ref.shape[0]):
        message = in_ref[i].astype(F32)
        side = jnp.concatenate([message[:, MSG - HEAD :]] * ROWS, axis=0)
        held.append([*(joined(message, h) for h in range(GROUP)), side])
    for o in range(out_ref.shape[0]):
        tiles = [jnp.zeros((TILE, HEAD), F32)] * (GROUP + 1)
        for i, message in enumerate(held):
            at = place_of(i, o)
            mine = jnp.broadcast_to(pick_ref[at : at + 1], (TILE, HEAD)) > 0.5
            tiles = [jnp.where(mine, m, tile) for m, tile in zip(message, tiles)]
        halves = [t[r * STEPS : (r + 1) * STEPS] for t in tiles[:GROUP] for r in range(ROWS)]
        out_ref[o] = jnp.concatenate([*halves, tiles[GROUP][:STEPS]], axis=1).astype(BF16)


def place_out_kernel(pick_ref, in_ref, out_ref):
    place(pick_ref, in_ref, out_ref, lambda y, s: s * in_ref.shape[0] + y)


def place_back_kernel(pick_ref, in_ref, out_ref):
    place(pick_ref, in_ref, out_ref, lambda s, y: s * out_ref.shape[0] + y)


def merged(in_ref):
    total = in_ref[0].astype(F32)
    for i in range(1, in_ref.shape[0]):
        total = total + in_ref[i].astype(F32)
    return total


def pieces(x, count):
    found = []
    for _ in range(count):
        piece = x.astype(BF16).astype(F32)
        found.append(piece)
        x = x - piece
    return found


def lent_kernel(in_ref, k_ref, v_ref, out_ref):
    message = merged(in_ref)
    q = jnp.concatenate([joined(message, h) for h in range(GROUP)], axis=0).astype(BF16)
    fills = by_request(message[:, MSG - HEAD :], k_ref.shape[0])
    block_len = k_ref.shape[1]
    k = k_ref[...].reshape(-1, HEAD)
    v = v_ref[...].reshape(-1, HEAD)
    s = dot_t(q, k) * SCALE
    lane = tile_iota(1).astype(F32)
    scores, valid = [], []
    for p in range(k_ref.shape[0]):
        scores.append(s[:, p * block_len : (p + 1) * block_len])
        valid.append(per_head(lane < fills[:, p : p + 1]))
    top, total, weights = soft_part(scores, valid)
    wide = jnp.concatenate([w.astype(BF16) for w in weights], axis=1)
    acc = jnp.dot(wide, v, preferred_element_type=F32)
    acc = acc * jnp.where(total > 0.0, 1.0 / jnp.maximum(total, 1e-30), 0.0)
    side = jnp.zeros((TILE, HEAD), F32)
    for h in range(GROUP):
        span = slice(h * TILE, (h + 1) * TILE)
        values = pieces(top[span], PARTS_M) + pieces(total[span], PARTS_L)
        for i, value in enumerate(values):
            side = jnp.where(tile_iota(1) == h * ROWS * PIECES + i, value, side)
    side = side[:STEPS] + pltpu.roll(side, PIECES, axis=1)[STEPS:]
    tiles = [acc[i * STEPS : (i + 1) * STEPS] for i in range(GROUP * ROWS)]
    reply = jnp.concatenate([*tiles, side], axis=1).astype(BF16)
    for i in range(out_ref.shape[0]):
        out_ref[i] = reply


def project_kernel(in_ref, o_ref, m_ref, l_ref, w_ref, out_ref):
    reply = merged(in_ref)
    side = by_request(reply[:, MSG - HEAD :], PIECES)
    heads = []
    for h in range(GROUP):
        span = slice(h * TILE, (h + 1) * TILE)
        first = h * ROWS * PIECES
        cols = [side[:, first + i : first + i + 1] for i in range(PIECES)]
        lent_top = cols[0] + cols[1] + cols[2]
        lent_total = cols[3] + cols[4]
        top = jnp.maximum(m_ref[span], lent_top)
        a = jnp.exp(m_ref[span] - top)
        b = jnp.exp(lent_top - top) * lent_total
        mixed = (a * o_ref[span] + b * joined(reply, h)) / (a * l_ref[span] + b)
        heads.append(mixed.astype(BF16))
    attended = jnp.concatenate(heads, axis=1)
    width = out_ref.shape[2]
    terms = jnp.dot(attended, w_ref[...], preferred_element_type=F32)
    for i, x in enumerate(SHARD):
        out_ref[i] = terms[:, x * width : (x + 1) * width]


def solution(mesh):
    insts, shards = mesh.shape["inst"], mesh.shape["tp"]
    per_row, lines = len(ROW), len(LINE)
    along_y = [[y * per_row + c for y in LINE] for c in range(per_row)]
    along_row = [[y * per_row + c for c in ROW] for y in range(lines)]

    def exchange(x, groups):
        return lax.all_to_all(x, "inst", 0, 0, axis_index_groups=groups, tiled=True)

    def local(
        queries,
        new_keys,
        new_values,
        res_keys,
        res_values,
        lendable_keys,
        lendable_values,
        ctx_len,
        blocks,
        lender,
        out_proj,
    ):
        def slots(n):
            return jax.ShapeDtypeStruct((n, STEPS, MSG), BF16)

        def like(x, space=pltpu.VMEM):
            return space(x.shape, x.dtype)

        def out_like(x):
            return jax.ShapeDtypeStruct(x.shape, x.dtype)

        numbers = (ctx_len, blocks, lender)
        given = (queries, new_keys, new_values, res_keys, res_values)
        lent = (lendable_keys, lendable_values)
        part = jax.ShapeDtypeStruct((QROWS, HEAD), F32)
        picks = jax.ShapeDtypeStruct((insts, HEAD), F32)
        outs = (slots(lines), part, part, part, picks, *map(out_like, lent))
        scratch = [
            *(like(x, pltpu.SMEM) for x in numbers),
            *map(like, given),
            pltpu.SemaphoreType.DMA((10,)),
        ]
        sent, *home, picked, lent_k, lent_v = call(first_kernel, outs, [HBM] * 10, scratch)(
            *map(off_chip, (*numbers, *given, *lent))
        )
        held = exchange(sent, along_y)
        placed = call(place_out_kernel, slots(per_row), [VMEM] * 2)(picked, held)
        arrived = exchange(placed, along_row)
        reply = call(lent_kernel, slots(per_row), [VMEM] * 3)(
            arrived, lent_k, lent_v
        )
        held_back = exchange(reply, along_row)
        placed_back = call(place_back_kernel, slots(lines), [VMEM] * 2)(picked, held_back)
        returned = exchange(placed_back, along_y)
        width = out_proj.shape[1] // shards
        terms = call(
            project_kernel,
            jax.ShapeDtypeStruct((shards, TILE, width), F32),
            [VMEM] * 5,
        )(returned, *home, out_proj)
        shares = lax.all_to_all(
            terms, "tp", 0, 0, axis_index_groups=[list(SHARD)], tiled=True
        )
        return jnp.sum(shares, axis=0).astype(BF16).reshape(ROWS, STEPS, width)

    in_specs = (
        P("inst", None, "tp"),
        P("inst", None, "tp"),
        P("inst", None, "tp"),
        P("inst", None, "tp"),
        P("inst", None, "tp"),
        P("inst", None, "tp"),
        P("inst", None, "tp"),
        P("inst"),
        P("inst", None),
        P(),
        P("tp", None),
    )
    out_specs = P("inst", None, "tp")
    return jax.shard_map(local, mesh=mesh, in_specs=in_specs, out_specs=out_specs, check_vma=False)
```
